256 devices in a mesh: section: 4 (over x_hi, core), tensor: 8 (over z), dp: 8 (over x_lo, y).
Axes of the slice: x: 4 (x_hi: 2, x_lo: 2; x = x_hi * 2 + x_lo), y: 4, z: 8, core: 2. Of those that a mesh axis runs over, the one named last changes fastest.
Arguments:
- act_inbox: bfloat16 [4, 4096, 16384], P('section', 'dp', 'tensor'), may hold values from -6 to 6
- grad_inbox: bfloat16 [4, 4096, 16384], P('section', 'dp', 'tensor'), may hold values from -0.0625 to 0.0625
- queries: bfloat16 [4, 4096, 16384], P('section', 'dp', 'tensor'), may hold values from -400 to 400
- keys_values: bfloat16 [4, 2, 4096, 1024], P('section', None, 'dp', 'tensor'), may hold values from -6 to 6
- saved_attn: bfloat16 [4, 4096, 16384], P('section', 'dp', 'tensor'), may hold values from -6 to 6
- down_adapt: bfloat16 [4, 8, 16, 16384], P('section', None, None, 'tensor'), may hold values from -0.375 to 0.375
- up_adapt: bfloat16 [4, 8, 16, 16384], P('section', None, None, 'tensor'), may hold values from -0.75 to 0.75
- seg_blocks: int32 [4, 2, 8, 3], P('section', None, 'dp'), may hold values from 1 to 4, 8 in all within a row
- seg_pads: int32 [4, 2, 8, 3], P('section', None, 'dp'), may hold values from 0 to 63
- seg_tenant: int32 [4, 2, 8, 3], P('section', None, 'dp'), may hold values from 0 to 31
- adapter_table: int32 [32], replicated, may hold values from 0 to 7
Outputs:
- new_acts: bfloat16 [4, 4096, 16384], P('section', 'dp', 'tensor')
- grad_down: bfloat16 [4, 8, 16, 16384], P('section', None, None, 'tensor')
- grad_up: bfloat16 [4, 8, 16, 16384], P('section', None, None, 'tensor')
The draws below stay inside these ranges and needn't reach their ends.
Inputs may be any that keep to these rules, and one draw needn't show every extreme that they name: `seg_blocks`: each row of 3 block counts sums to 8.
All inputs are finite; a program needn't handle non-finite values.
Results may differ from the reference program's by a relative error of at most 0.0058.
Values may be sent and summed in bfloat16 or wider, within the bound.
No kernel may reach another device: no remote copies, remote signals or barrier semaphores. Data moves between devices by JAX's collectives and lax.ppermute only.
A program may use at most 128 MiB of HBM per device.

```python
import math
import jax
import jax.numpy as jnp
import numpy as np
from jax import lax

HQ = 128
KVH = 8
HD = 128
MODEL_WIDTH = 16384
ADAPTER_RANK = 16
ADAPTER_COUNT = 8
TENANTS = 32
BLOCK = 64
SEGS = 3
TOK_DEV = 512
TOKENS = 4096
N_SECTION = 4
N_DP = 8


def key_field(key):
    return jax.random.truncated_normal(key, -6.0, 6.0, (N_SECTION, TOKENS, KVH * HD), jnp.float32)


def draw_keys_values(key, part):
    key_part = key_field(key)
    key = jax.random.fold_in(key, 3)
    value_part = jax.random.truncated_normal(key, -6.0, 6.0, (N_SECTION, TOKENS, KVH * HD), jnp.float32)
    return jnp.stack([key_part, value_part], axis=1).astype(jnp.bfloat16)


def draw_queries(key, part):
    key = jax.random.fold_in(key, 5)
    first = jax.random.fold_in(key, 0)
    field = jax.random.truncated_normal(first, -6.0, 6.0, (N_SECTION, TOKENS, HQ, HD), jnp.float32)
    return field.reshape(N_SECTION, TOKENS, HQ * HD).astype(jnp.bfloat16)


def touch_ends(drawn, own_key, low, high):
    place = [jax.random.randint(jax.random.fold_in(own_key, axis), (), 0, length) for axis, length in enumerate(drawn.shape)]
    main_axis = drawn.shape.index(max(drawn.shape))
    beside = place[:main_axis] + [(place[main_axis] + 1) % drawn.shape[main_axis]] + place[main_axis + 1:]
    return drawn.at[tuple(place)].set(low).at[tuple(beside)].set(high)


def shard_levels(own_key, shape, cuts, smallest, largest):
    level, own = 1.0, jax.random.fold_in(own_key, 6)
    for dim, shards_of in cuts:
        heights = jnp.exp(jax.random.uniform(jax.random.fold_in(own, dim), (shards_of,), jnp.float32, smallest / len(cuts), largest / len(cuts)))
        level = level * jnp.repeat(heights, shape[dim] // shards_of).reshape([-1 if axis == dim else 1 for axis in range(len(shape))])
    return level


def rank_bounds(amount, lean):
    weights = [(1 << 20) // math.isqrt(standing ** lean) + 1 for standing in range(1, amount + 1)]
    width = 1 + sum(weights) // (1 << 30)
    return np.cumsum(np.array([max(1, weight // width) for weight in weights]))


def skewed_ids(rng, extent, number_of, slope):
    grid = rank_bounds(number_of, slope)
    pick = jax.random.randint(jax.random.fold_in(rng, 1), extent, 0, int(grid[number_of - 1]))
    rank = jnp.searchsorted(jnp.asarray(grid, jnp.int32), pick, side="right")
    return jax.random.permutation(jax.random.fold_in(rng, 2), number_of)[rank].astype(jnp.int32)


def profile(count, total, reach, lean):
    loads = [(1 << 20) // math.isqrt(grade ** lean) + 1 for grade in range(2, count + 1)]
    surplus, counts = total - reach - (count - 1), [1] * (count - 1)
    while surplus > 0:
        candidates = [i for i in range(count - 1) if counts[i] < reach]
        whole, left = sum([loads[i] for i in candidates]), surplus
        for i in candidates:
            extra = min(reach - counts[i], max(1, left * loads[i] // whole), surplus)
            counts[i] = counts[i] + extra
            surplus = surplus - extra
    return np.array([reach] + counts)


def ragged(rng, count, total, most, skew):
    if count == 2:
        one = jax.random.randint(rng, (), max(1, total - most), min(most, total - 1) + 1)
        return jnp.stack([one, total - one])
    tallies = jnp.asarray(profile(count, total, most, skew), jnp.int32)
    couples = (count - 1) // 2
    source_of, receiver = tallies[1:1 + 2 * couples:2], tallies[2:2 + 2 * couples:2]
    slack = jnp.minimum(source_of - 1, most - receiver)
    passed = jax.random.randint(jax.random.fold_in(rng, 1), (couples,), 0, 1 << 20) % (slack + 1)
    tallies = tallies.at[1:1 + 2 * couples:2].set(source_of - passed).at[2:2 + 2 * couples:2].set(receiver + passed)
    return tallies[jax.random.permutation(jax.random.fold_in(rng, 2), count)]


def gaussian(key, dims, scale, limit, shards=(), kind=jnp.bfloat16):
    array = jax.random.normal(key, dims, jnp.float32) * scale
    if len(shards) > 0:
        array = shard_levels(key, dims, shards, -0.22, 0.18) * array
    return jnp.clip(array, min=-limit, max=limit).astype(kind)


def setup_inputs(seed: int = 0) -> dict:
    keys = jax.random.split(jax.random.key(seed), 12)
    return {
        "act_inbox": gaussian(keys[0], (N_SECTION, TOKENS, MODEL_WIDTH), 1.0, 6.0, ((0, 4), (1, 8), (2, 8))),
        "grad_inbox": gaussian(keys[1], (N_SECTION, TOKENS, MODEL_WIDTH), ((TOK_DEV * N_DP) ** -0.5 / 4), 0.0625, ((0, 4), (1, 8), (2, 8))),
        "queries": draw_queries(jax.random.fold_in(keys[11], 71), 0),
        "keys_values": draw_keys_values(jax.random.fold_in(keys[11], 71), 0),
        "saved_attn": gaussian(keys[4], (N_SECTION, TOKENS, MODEL_WIDTH), 1.0, 6.0, ((0, 4), (1, 8), (2, 8))),
        "down_adapt": gaussian(keys[5], (N_SECTION, ADAPTER_COUNT, ADAPTER_RANK, MODEL_WIDTH), (MODEL_WIDTH // 64) ** -0.5, 0.375, ((0, 4), (3, 8))),
        "up_adapt": gaussian(keys[6], (N_SECTION, ADAPTER_COUNT, ADAPTER_RANK, MODEL_WIDTH), 64 ** -0.5, 0.75, ((0, 4), (3, 8))),
        "seg_blocks": jax.vmap(lambda own: ragged(own, SEGS, TOK_DEV // BLOCK, TOK_DEV // (2 * BLOCK), 0))(jax.random.split(keys[7], N_SECTION * 2 * N_DP)).reshape((N_SECTION, 2, N_DP, SEGS)).astype(jnp.int32),
        "seg_pads": touch_ends(jax.random.randint(keys[8], (N_SECTION, 2, N_DP, SEGS), 0, BLOCK), jax.random.fold_in(keys[8], 1), 0, BLOCK - 1).astype(jnp.int32),
        "seg_tenant": touch_ends(skewed_ids(keys[9], (N_SECTION, 2, N_DP, SEGS), TENANTS, 2), jax.random.fold_in(keys[9], 3), 0, TENANTS - 1).astype(jnp.int32),
        "adapter_table": touch_ends(jax.random.randint(keys[10], (TENANTS,), 0, ADAPTER_COUNT), jax.random.fold_in(keys[10], 1), 0, ADAPTER_COUNT - 1).astype(jnp.int32),
    }


adapter_scale = 2.0

def token_layout(blocks, padding, tenants, slot_table):
    positions = jnp.arange(TOK_DEV, dtype=jnp.int32)
    seg_ends = jnp.cumsum(blocks).astype(jnp.int32) * BLOCK
    segment = lax.optimization_barrier(jnp.sum((positions[:, None] >= seg_ends[None, :]).astype(jnp.int32), axis=1))
    member = (segment[:, None] == jnp.arange(SEGS, dtype=jnp.int32)[None, :]).astype(jnp.int32)
    live_end = lax.optimization_barrier(jnp.sum(member * (seg_ends - padding)[None, :], axis=1))
    alive = positions < live_end
    tenant_pick = (tenants[:, None] == jnp.arange(TENANTS, dtype=jnp.int32)[None, :]).astype(jnp.int32)
    seg_slot = lax.optimization_barrier(jnp.sum(tenant_pick * slot_table[None, :], axis=1))
    token_slot = lax.optimization_barrier(jnp.sum(member * seg_slot[None, :], axis=1))
    onehot = (token_slot[:, None] == jnp.arange(ADAPTER_COUNT, dtype=jnp.int32)[None, :]).astype(jnp.float32)
    return (segment, alive, onehot)

def attend(queries, keys_values, segment, alive):
    length = queries.shape[0]
    group_size = HQ // KVH
    query_heads = queries.astype(jnp.float32).reshape(length, KVH, group_size, HD)
    key_heads = keys_values[0].astype(jnp.float32).reshape(length, KVH, HD)
    value_heads = keys_values[1].astype(jnp.float32).reshape(length, KVH, HD)
    block_rows = length if length <= 1024 else 512
    positions = jnp.arange(length, dtype=jnp.int32)
    inv_root = 1.0 / math.sqrt(HD)

    def one_block(block_index):
        block_start = block_index * block_rows
        block_q = lax.dynamic_slice_in_dim(query_heads, block_start, block_rows, 0)
        block_pos = block_start + jnp.arange(block_rows, dtype=jnp.int32)
        block_seg = lax.dynamic_slice_in_dim(segment, block_start, block_rows, 0)
        block_live = lax.dynamic_slice_in_dim(alive, block_start, block_rows, 0)
        scores = jnp.einsum('qhgd,khd->hgqk', block_q, key_heads) * inv_root
        allowed = (block_seg[:, None] == segment[None, :]) & (block_pos[:, None] >= positions[None, :])
        allowed = allowed & alive[None, :] & block_live[:, None]
        masked_scores = jnp.where(allowed, scores, -1e+30)
        row_top = lax.optimization_barrier(jnp.max(masked_scores, axis=-1, keepdims=True))
        exponent = jnp.where(allowed, jnp.exp(masked_scores - row_top), 0.0)
        row_total = lax.optimization_barrier(jnp.sum(exponent, axis=-1, keepdims=True))
        row_total = jnp.where(block_live[None, None, :, None], row_total, 1.0)
        weights = (exponent / row_total).astype(jnp.bfloat16)
        attended = jnp.einsum('hgqk,khd->qhgd', weights.astype(jnp.float32), value_heads)
        return attended.astype(jnp.bfloat16).reshape(block_rows, HQ * HD)
    blocks_out = lax.map(one_block, jnp.arange(length // block_rows, dtype=jnp.int32))
    return blocks_out.reshape(length, HQ * HD)

def project_rows(left, right):
    return lax.dot_general(left, right, (((1,), (1,)), ((), ())), preferred_element_type=jnp.float32)

def contract(left, right):
    return lax.dot_general(left, right, (((0,), (0,)), ((), ())), preferred_element_type=jnp.float32)

def select_slots(full, onehot):
    return lax.optimization_barrier(jnp.sum(full.reshape(full.shape[0], onehot.shape[1], -1) * onehot[:, :, None], axis=1))

def spread_tokens(ranked, onehot):
    wide = onehot[:, :, None] * ranked.astype(jnp.float32)[:, None, :]
    return wide.reshape(ranked.shape[0], -1).astype(jnp.bfloat16)

def reference(act_inbox, grad_inbox, queries, keys_values, saved_attn, down_adapt, up_adapt, seg_blocks, seg_pads, seg_tenant, adapter_table):
    received_input = jnp.roll(act_inbox, 1, axis=0)
    returned = jnp.roll(grad_inbox, -1, axis=0)
    acts_all, downs_all, every_up_weight = ([], [], [])
    for relay_section_index in range(N_SECTION):
        down_rows = down_adapt[relay_section_index].reshape(ADAPTER_COUNT * ADAPTER_RANK, MODEL_WIDTH)
        upward_rows = up_adapt[relay_section_index].reshape(ADAPTER_COUNT * ADAPTER_RANK, MODEL_WIDTH)
        pieces = []
        grad_d = jnp.zeros((ADAPTER_COUNT * ADAPTER_RANK, MODEL_WIDTH), jnp.float32)
        up_gradient = jnp.zeros((ADAPTER_COUNT * ADAPTER_RANK, MODEL_WIDTH), jnp.float32)
        for group_index in range(N_DP):
            starting_row = group_index * TOK_DEV
            ending_row = starting_row + TOK_DEV
            segment, alive, onehot = token_layout(seg_blocks[relay_section_index, 0, group_index], seg_pads[relay_section_index, 0, group_index], seg_tenant[relay_section_index, 0, group_index], adapter_table)
            attended = attend(queries[relay_section_index, starting_row:ending_row], keys_values[relay_section_index, :, starting_row:ending_row], segment, alive)
            fwd_rank = select_slots(project_rows(attended, down_rows), onehot).astype(jnp.bfloat16)
            adapter_update = jnp.dot(spread_tokens(fwd_rank, onehot), upward_rows, preferred_element_type=jnp.float32)
            summed_output = received_input[relay_section_index, starting_row:ending_row].astype(jnp.float32) + adapter_scale * adapter_update
            pieces.append(summed_output.astype(jnp.bfloat16))
            back_seg, back_alive, backward_slot_mask = token_layout(seg_blocks[relay_section_index, 1, group_index], seg_pads[relay_section_index, 1, group_index], seg_tenant[relay_section_index, 1, group_index], adapter_table)
            saved_rows = saved_attn[relay_section_index, starting_row:ending_row]
            masked_scores = returned[relay_section_index, starting_row:ending_row] * back_alive[:, None].astype(jnp.bfloat16)
            back_rank = select_slots(project_rows(saved_rows, down_rows), backward_slot_mask).astype(jnp.bfloat16)
            backward_gradient = (adapter_scale * select_slots(project_rows(masked_scores, upward_rows), backward_slot_mask)).astype(jnp.bfloat16)
            up_gradient = up_gradient + contract(spread_tokens(back_rank, backward_slot_mask), masked_scores)
            grad_d = grad_d + contract(spread_tokens(backward_gradient, backward_slot_mask), saved_rows)
        acts_all.append(jnp.concatenate(pieces, axis=0))
        downs_all.append(grad_d.reshape(ADAPTER_COUNT, ADAPTER_RANK, MODEL_WIDTH).astype(jnp.bfloat16))
        every_up_weight.append((adapter_scale * up_gradient).reshape(ADAPTER_COUNT, ADAPTER_RANK, MODEL_WIDTH).astype(jnp.bfloat16))
    return (jnp.stack(acts_all), jnp.stack(downs_all), jnp.stack(every_up_weight))
```

```python
import math

import jax
import jax.numpy as jnp
from jax import lax
from jax.experimental import pallas as pl
from jax.experimental.pallas import tpu as pltpu
from jax.sharding import PartitionSpec as P

HD = 128
BLOCK = 64
SEGS = 3
MOST_BLOCKS = 4
ADAPTER_SCALE = 2.0
BF16 = jnp.bfloat16
F32 = jnp.float32
SMEM = pl.BlockSpec(memory_space=pltpu.SMEM)
VMEM = pl.BlockSpec(memory_space=pltpu.VMEM)
PARAMS = pltpu.CompilerParams(vmem_limit_bytes=48 * 1024 * 1024)


def cost(flops, size, exps=0):
    return pl.CostEstimate(flops=flops, bytes_accessed=size, transcendentals=exps)


def rows_by_rows(left, right):
    return lax.dot_general(left, right, (((1,), (1,)), ((), ())), preferred_element_type=F32)


def segments(blocks, pads, tenants, table, batch):
    starts, lives, slots = [], [], []
    start = jnp.int32(0)
    for i in range(SEGS):
        end = start + blocks[0, batch, 0, i] * BLOCK
        starts.append(start)
        lives.append(end - pads[0, batch, 0, i])
        slots.append(table[tenants[0, batch, 0, i]])
        start = end
    return starts, lives, slots


def alive_rows(starts, lives, first, count):
    token = first + lax.broadcasted_iota(jnp.int32, (1, count), 1)
    return [(token >= s) & (token < e) for s, e in zip(starts, lives)]


def pick_rows(adapters, slots):
    return jnp.concatenate([adapters[0, s] for s in slots], axis=0)


def fold(full, masks, rank):
    return sum(jnp.where(m, full[rank * i : rank * (i + 1)], 0.0) for i, m in enumerate(masks))


def spread(ranked, masks):
    wide = ranked.astype(F32)
    return jnp.concatenate([jnp.where(m, wide, 0.0) for m in masks], axis=0).astype(BF16)


def prepare_kernel(blocks, pads, tenants, table, saved, down, up, out):
    rank, length = up.shape[2], saved.shape[1]
    starts, lives, slots = segments(blocks, pads, tenants, table, 1)
    wide = SEGS * rank
    for i in range(SEGS):
        out[rank * i : rank * (i + 1), :] = up[0, slots[i]]
    masks = alive_rows(starts, lives, 0, length)
    row = lax.broadcasted_iota(jnp.int32, (rank, length), 0)
    notes = jnp.zeros((rank, length), F32)
    for i in range(SEGS):
        notes = jnp.where((row == i) & masks[i], 1.0, notes)
        notes = jnp.where(row == SEGS + i, slots[i].astype(F32), notes)
    back = fold(rows_by_rows(pick_rows(down, slots), saved[0]), masks, rank)
    out[wide:, :length] = notes.astype(BF16)
    out[wide:, length : 2 * length] = back.astype(BF16)
    out[wide:, 2 * length :] = jnp.zeros((rank, out.shape[1] - 2 * length), BF16)


def note_masks(ahead, wide, length):
    notes = ahead[wide:, :length].astype(F32)
    return [notes[i : i + 1] > 0.5 for i in range(SEGS)]


def back_gradient_kernel(ahead, grads, out):
    rank, length = out.shape
    wide = SEGS * rank
    full = rows_by_rows(ahead[:wide, :], grads[0])
    out[...] = fold(full, note_masks(ahead, wide, length), rank).astype(BF16)


def attention_kernel(blocks, pads, tenants, table, queries, keys_values, down, out, attended):
    rank, length = out.shape
    heads = queries.shape[2] // HD
    starts, lives, slots = segments(blocks, pads, tenants, table, 0)
    power = math.log2(math.e) / math.sqrt(HD)
    for j in range(length // BLOCK):
        low, high = max(0, j + 1 - MOST_BLOCKS) * BLOCK, (j + 1) * BLOCK
        here = slice(j * BLOCK, high)
        start, live = starts[0], lives[0]
        for i in range(1, SEGS):
            inside = j * BLOCK >= starts[i]
            start = jnp.where(inside, starts[i], start)
            live = jnp.where(inside, lives[i], live)
        query_at = j * BLOCK + lax.broadcasted_iota(jnp.int32, (BLOCK, high - low), 0)
        key_at = low + lax.broadcasted_iota(jnp.int32, (BLOCK, high - low), 1)
        seen = ((key_at <= query_at) & (key_at >= start))[None]
        alive = (j * BLOCK + lax.broadcasted_iota(jnp.int32, (BLOCK, 1), 0) < live)[None]
        stacked = jnp.concatenate(
            [queries[0, here, HD * h : HD * (h + 1)] for h in range(heads)], axis=0
        )
        scores = rows_by_rows(stacked, keys_values[0, 0, low:high, :])
        scores = jnp.where(seen, scores.reshape(heads, BLOCK, high - low), -1e30)
        top = jnp.max(scores, axis=-1, keepdims=True)
        exponent = jnp.exp2((scores - top) * power)
        total = jnp.sum(exponent, axis=-1, keepdims=True)
        weights = (exponent * jnp.where(alive, 1.0 / total, 0.0)).astype(BF16)
        mixed = jnp.dot(
            weights.reshape(heads * BLOCK, high - low),
            keys_values[0, 1, low:high, :],
            preferred_element_type=F32,
        ).astype(BF16)
        for h in range(heads):
            attended[here, HD * h : HD * (h + 1)] = mixed[BLOCK * h : BLOCK * (h + 1)]
    full = rows_by_rows(pick_rows(down, slots), attended[...])
    out[...] = fold(full, alive_rows(starts, lives, 0, length), rank).astype(BF16)


def contract_kernel(blocks, pads, tenants, table, parts, ahead, saved, grads, fwd, out):
    rank, length = fwd.shape
    wide = SEGS * rank
    starts, lives, slots = segments(blocks, pads, tenants, table, 1)
    total = jnp.sum(parts[...].astype(F32), axis=0)
    fwd[...] = total[:rank].astype(BF16)
    back_rank = total[rank : 2 * rank].astype(BF16)
    back_grad = (ADAPTER_SCALE * total[2 * rank :]).astype(BF16)
    down_part = jnp.dot(
        spread(back_grad, alive_rows(starts, lives, 0, length)), saved[0], preferred_element_type=F32
    ).astype(BF16)
    up_part = jnp.dot(
        spread(back_rank, note_masks(ahead, wide, length)), grads[0], preferred_element_type=F32
    ).astype(BF16)
    count, _, width = out.shape
    row = lax.broadcasted_iota(jnp.int32, (rank, width), 0)
    notes = ahead[wide:, :width].astype(F32)
    for i in range(SEGS):
        notes = jnp.where(row == i, slots[i].astype(F32), notes)
    for d in range(count):
        out[d, :wide, :] = down_part[:, width * d : width * (d + 1)]
        out[d, wide : 2 * wide, :] = up_part[:, width * d : width * (d + 1)]
        out[d, 2 * wide :, :] = notes.astype(BF16)


def collect_kernel(pieces, down_out, up_out):
    count, _, width = pieces.shape
    rows = down_out.shape[0]
    rank = pieces.shape[1] // (2 * SEGS + 1)
    wide = SEGS * rank
    slot_at = lax.broadcasted_iota(jnp.int32, (rows // rank, 1, width), 0).astype(F32)
    for half, ref, scale in ((0, down_out, 1.0), (1, up_out, ADAPTER_SCALE)):
        total = jnp.zeros((rows // rank, rank, width), F32)
        for d in range(count):
            notes = pieces[d, 2 * wide :, :].astype(F32)
            for i in range(SEGS):
                slot = notes[half * SEGS + i : half * SEGS + i + 1]
                first = half * wide + rank * i
                piece = pieces[d, first : first + rank, :].astype(F32)
                total = total + jnp.where(slot_at == slot[None], piece[None], 0.0)
        ref[...] = (scale * total).reshape(rows, width).astype(BF16)


def hand_on_kernel(blocks, pads, tenants, table, arrived, fwd, up, out):
    rows = out.shape[1]
    first = pl.multiple_of(pl.program_id(0) * rows, rows)
    starts, lives, slots = segments(blocks, pads, tenants, table, 0)
    wide = spread(fwd[:, pl.ds(first, rows)], alive_rows(starts, lives, first, rows))
    update = lax.dot_general(
        wide, pick_rows(up, slots), (((0,), (0,)), ((), ())), preferred_element_type=F32
    )
    out[0] = (arrived[0].astype(F32) + ADAPTER_SCALE * update).astype(BF16)


def shift(value, steps):
    count = lax.axis_size("section")
    return lax.ppermute(value, "section", [(i, (i + steps) % count) for i in range(count)])


def per_device(
    act_inbox,
    grad_inbox,
    queries,
    keys_values,
    saved_attn,
    down_adapt,
    up_adapt,
    seg_blocks,
    seg_pads,
    seg_tenant,
    adapter_table,
):
    _, length, width = act_inbox.shape
    _, slot_count, rank, _ = up_adapt.shape
    wide = SEGS * rank
    scalars = (seg_blocks, seg_pads, seg_tenant, adapter_table)
    tensor_count, dp_count = lax.axis_size("tensor"), lax.axis_size("dp")
    part = width // dp_count
    piece = length * width * 2

    ahead = pl.pallas_call(
        prepare_kernel,
        out_shape=jax.ShapeDtypeStruct((wide + rank, width), BF16),
        in_specs=[SMEM] * 4 + [VMEM] * 3,
        out_specs=VMEM,
        compiler_params=PARAMS,
        cost_estimate=cost(2 * wide * length * width, piece * 3 // 2),
        name="prepare",
    )(*scalars, saved_attn, down_adapt, up_adapt)
    ahead = shift(ahead, 1)
    arrived = shift(act_inbox, 1)

    fwd_part = pl.pallas_call(
        attention_kernel,
        out_shape=jax.ShapeDtypeStruct((rank, length), BF16),
        in_specs=[SMEM] * 4 + [VMEM] * 3,
        out_specs=VMEM,
        scratch_shapes=[pltpu.VMEM((length, width), BF16)],
        compiler_params=PARAMS,
        cost_estimate=cost(
            4 * length * MOST_BLOCKS * BLOCK * width + 2 * wide * length * width,
            piece * 3 // 2,
            length * MOST_BLOCKS * BLOCK * width // HD,
        ),
        name="attention",
    )(*scalars, queries, keys_values, down_adapt)

    grad_part = pl.pallas_call(
        back_gradient_kernel,
        out_shape=jax.ShapeDtypeStruct((rank, length), BF16),
        in_specs=[VMEM] * 2,
        out_specs=VMEM,
        compiler_params=PARAMS,
        cost_estimate=cost(2 * wide * length * width, piece),
        name="back_gradient",
    )(ahead, grad_inbox)
    grad_part = shift(grad_part, -1)

    parts = jnp.concatenate([fwd_part, ahead[wide:, length : 2 * length], grad_part], axis=0)
    parts = jnp.broadcast_to(parts[None], (tensor_count, *parts.shape))
    parts = lax.all_to_all(parts, "tensor", 0, 0)

    fwd_rank, pieces = pl.pallas_call(
        contract_kernel,
        out_shape=(
            jax.ShapeDtypeStruct((rank, length), BF16),
            jax.ShapeDtypeStruct((dp_count, 2 * wide + rank, part), BF16),
        ),
        in_specs=[SMEM] * 4 + [VMEM] * 4,
        out_specs=(VMEM, VMEM),
        compiler_params=PARAMS,
        cost_estimate=cost(4 * wide * length * width, 2 * piece),
        name="contract",
    )(*scalars, parts, ahead, saved_attn, grad_inbox)
    pieces = lax.all_to_all(pieces, "dp", 0, 0)

    down_sum, up_sum = pl.pallas_call(
        collect_kernel,
        out_shape=(jax.ShapeDtypeStruct((slot_count * rank, part), BF16),) * 2,
        in_specs=[VMEM],
        out_specs=(VMEM, VMEM),
        compiler_params=PARAMS,
        cost_estimate=cost(4 * dp_count * SEGS * slot_count * rank * part, piece // 4),
        name="collect",
    )(pieces)
    up_sum = shift(up_sum, -1)

    rows = 128
    new_acts = pl.pallas_call(
        hand_on_kernel,
        grid=(length // rows,),
        out_shape=jax.ShapeDtypeStruct(act_inbox.shape, BF16),
        in_specs=[SMEM] * 4 + [pl.BlockSpec((1, rows, width), lambda i: (0, i, 0)), VMEM, VMEM],
        out_specs=pl.BlockSpec((1, rows, width), lambda i: (0, i, 0)),
        compiler_params=PARAMS,
        cost_estimate=cost(2 * wide * length * width, 2 * piece),
        name="hand_on",
    )(*scalars, arrived, fwd_rank, up_adapt)

    sums = jnp.concatenate([down_sum, up_sum], axis=0)
    sums = jnp.broadcast_to(sums[None], (dp_count, *sums.shape))
    sums = lax.all_to_all(sums, "dp", 0, 0)
    sums = sums.transpose(1, 0, 2).reshape(2, 1, slot_count, rank, width)
    return new_acts, sums[0], sums[1]


def solution(mesh):
    placed = (
        P("section", "dp", "tensor"),
        P("section", "dp", "tensor"),
        P("section", "dp", "tensor"),
        P("section", None, "dp", "tensor"),
        P("section", "dp", "tensor"),
        P("section", None, None, "tensor"),
        P("section", None, None, "tensor"),
        P("section", None, "dp", None),
        P("section", None, "dp", None),
        P("section", None, "dp", None),
        P(),
    )
    return jax.shard_map(
        per_device,
        mesh=mesh,
        in_specs=placed,
        out_specs=(
            P("section", "dp", "tensor"),
            P("section", None, None, "tensor"),
            P("section", None, None, "tensor"),
        ),
        check_vma=False,
    )
```

```python
import math

import jax
import jax.numpy as jnp
from jax import lax
from jax.experimental import pallas as pl
from jax.experimental.pallas import tpu as pltpu
from jax.sharding import PartitionSpec as P

HD = 128
BLOCK = 64
SEGS = 3
MOST_BLOCKS = 4
ADAPTER_SCALE = 2.0
BF16 = jnp.bfloat16
F32 = jnp.float32
SMEM = pl.BlockSpec(memory_space=pltpu.SMEM)
VMEM = pl.BlockSpec(memory_space=pltpu.VMEM)
HBM = pl.BlockSpec(memory_space=pltpu.HBM)
PARAMS = pltpu.CompilerParams(vmem_limit_bytes=20 * 1024 * 1024)


def cost(flops, size, exps=0):
    return pl.CostEstimate(flops=flops, bytes_accessed=size, transcendentals=exps)


def rows_by_rows(left, right):
    return lax.dot_general(left, right, (((1,), (1,)), ((), ())), preferred_element_type=F32)


def segments(blocks, pads, tenants, table, batch):
    starts, lives, slots = [], [], []
    start = jnp.int32(0)
    for i in range(SEGS):
        end = start + blocks[0, batch, 0, i] * BLOCK
        starts.append(start)
        lives.append(end - pads[0, batch, 0, i])
        slots.append(table[tenants[0, batch, 0, i]])
        start = end
    return starts, lives, slots


def alive_rows(starts, lives, first, count):
    token = first + lax.broadcasted_iota(jnp.int32, (1, count), 1)
    return [(token >= s) & (token < e) for s, e in zip(starts, lives)]


def pick_rows(adapters, slots):
    return jnp.concatenate([adapters[0, s] for s in slots], axis=0)


def fold(full, masks, rank):
    return sum(jnp.where(m, full[rank * i : rank * (i + 1)], 0.0) for i, m in enumerate(masks))


def spread(ranked, masks):
    wide = ranked.astype(F32)
    return jnp.concatenate([jnp.where(m, wide, 0.0) for m in masks], axis=0).astype(BF16)


def prepare_kernel(blocks, pads, tenants, table, saved, down, up, out, info, raw, listed, held, downs, ups, sems):
    _, _, rank, width = up.shape
    length = saved.shape[1]
    wide = SEGS * rank
    cuts = sems.shape[0] - 6
    tall = length // cuts
    first = [pltpu.make_async_copy(src, raw.at[i], sems.at[i]) for i, src in enumerate((blocks, pads, tenants))]
    first.append(pltpu.make_async_copy(table, listed, sems.at[3]))
    adapters = [
        pltpu.make_async_copy(up, ups, sems.at[4]),
        pltpu.make_async_copy(down, downs, sems.at[5]),
    ]
    later = []
    for i in range(cuts):
        at = pl.ds(tall * i, tall)
        later.append(pltpu.make_async_copy(saved.at[0, at], held.at[at], sems.at[6 + i]))
    for copy in first + later + adapters:
        copy.start()
    for copy in first:
        copy.wait()
    for batch in range(2):
        found = segments(raw.at[0], raw.at[1], raw.at[2], listed, batch)
        for i, values in enumerate(found):
            for k, value in enumerate(values):
                info[0, SEGS * (SEGS * batch + i) + k] = value
    starts, lives, slots = found
    masks = alive_rows(starts, lives, 0, length)
    row = lax.broadcasted_iota(jnp.int32, (rank, length), 0)
    notes = jnp.zeros((rank, length), F32)
    for i in range(SEGS):
        notes = jnp.where((row == i) & masks[i], 1.0, notes)
        notes = jnp.where(row == SEGS + i, slots[i].astype(F32), notes)
    out[wide:, :length] = notes.astype(BF16)
    out[wide:, 2 * length :] = jnp.zeros((rank, width - 2 * length), BF16)
    adapters[0].wait()
    for i in range(SEGS):
        out[rank * i : rank * (i + 1), :] = ups[0, slots[i]]
    adapters[1].wait()
    rows = pick_rows(downs, slots)
    for i, copy in enumerate(later):
        copy.wait()
        at = slice(tall * i, tall * (i + 1))
        back = fold(rows_by_rows(rows, held[at]), [m[:, at] for m in masks], rank)
        out[wide:, length + tall * i : length + tall * (i + 1)] = back.astype(BF16)


def recall(info, batch):
    base = SEGS * SEGS * batch
    return [[info[0, base + SEGS * i + k] for k in range(SEGS)] for i in range(3)]


def note_masks(ahead, wide, length):
    notes = ahead[wide:, :length].astype(F32)
    return [notes[i : i + 1] > 0.5 for i in range(SEGS)]


def back_gradient_kernel(ahead, grads, out):
    rank, length = out.shape
    wide = SEGS * rank
    full = rows_by_rows(ahead[:wide, :], grads[0])
    out[...] = fold(full, note_masks(ahead, wide, length), rank).astype(BF16)


def attend_blocks(info, queries, keys_values, attended, first, last, base):
    heads = queries.shape[2] // HD
    starts, lives, _ = recall(info, 0)
    power = math.log2(math.e) / math.sqrt(HD)
    for j in range(first, last):
        low, high = max(0, j + 1 - MOST_BLOCKS) * BLOCK, (j + 1) * BLOCK
        here = slice(j * BLOCK, high)
        start, live = starts[0], lives[0]
        for i in range(1, SEGS):
            inside = j * BLOCK >= starts[i]
            start = jnp.where(inside, starts[i], start)
            live = jnp.where(inside, lives[i], live)
        query_at = j * BLOCK + lax.broadcasted_iota(jnp.int32, (BLOCK, high - low), 0)
        key_at = low + lax.broadcasted_iota(jnp.int32, (BLOCK, high - low), 1)
        seen = ((key_at <= query_at) & (key_at >= start))[None]
        alive = (j * BLOCK + lax.broadcasted_iota(jnp.int32, (BLOCK, 1), 0) < live)[None]
        stacked = jnp.concatenate(
            [queries[0, here, HD * h : HD * (h + 1)] for h in range(heads)], axis=0
        )
        scores = rows_by_rows(stacked, keys_values[0, 0, low:high, :])
        scores = jnp.where(seen, scores.reshape(heads, BLOCK, high - low), -1e30)
        top = jnp.max(scores, axis=-1, keepdims=True)
        exponent = jnp.exp2((scores - top) * power)
        total = jnp.sum(exponent, axis=-1, keepdims=True)
        weights = (exponent * jnp.where(alive, 1.0 / total, 0.0)).astype(BF16)
        mixed = jnp.dot(
            weights.reshape(heads * BLOCK, high - low),
            keys_values[0, 1, low:high, :],
            preferred_element_type=F32,
        ).astype(BF16)
        for h in range(heads):
            at = slice((j - base) * BLOCK, (j + 1 - base) * BLOCK)
            attended[at, HD * h : HD * (h + 1)] = mixed[BLOCK * h : BLOCK * (h + 1)]


def ranked_attention(info, down, attended, first, out):
    rank, length = out.shape
    starts, lives, slots = recall(info, 0)
    full = rows_by_rows(pick_rows(down, slots), attended[...])
    out[...] = fold(full, alive_rows(starts, lives, first, length), rank)


def early_attention_kernel(info, queries, keys_values, down, out, attended):
    attend_blocks(info, queries, keys_values, attended, 0, attended.shape[0] // BLOCK, 0)
    ranked_attention(info, down, attended, 0, out)


def late_attention_kernel(info, queries, keys_values, down, out, attended):
    half = attended.shape[0] // BLOCK
    attend_blocks(info, queries, keys_values, attended, half, 2 * half, half)
    ranked_attention(info, down, attended, half * BLOCK, out)


def contract_kernel(info, parts, ahead, saved, grads, out, held, sems):
    _, rows, length = parts.shape
    rank = rows // 2
    wide = SEGS * rank
    cuts = sems.shape[1]
    tall = length // cuts
    copies = []
    for k, ref in enumerate((saved, grads)):
        for i in range(cuts):
            at = pl.ds(tall * i, tall)
            copies.append(pltpu.make_async_copy(ref.at[0, at], held.at[k, at], sems.at[k, i]))
    for copy in copies:
        copy.start()
    starts, lives, slots = recall(info, 1)
    total = jnp.sum(parts[...].astype(F32), axis=0)
    back_rank = total[:rank].astype(BF16)
    back_grad = (ADAPTER_SCALE * total[rank:]).astype(BF16)
    count, _, width = out.shape
    row = lax.broadcasted_iota(jnp.int32, (rank, width), 0)
    notes = ahead[wide:, :width].astype(F32)
    for i in range(SEGS):
        notes = jnp.where(row == i, slots[i].astype(F32), notes)
    lefts = (
        spread(back_grad, alive_rows(starts, lives, 0, length)),
        spread(back_rank, note_masks(ahead, wide, length)),
    )
    for d in range(count):
        out[d, 2 * wide :, :] = notes.astype(BF16)
    for k, left in enumerate(lefts):
        for copy in copies[cuts * k : cuts * (k + 1)]:
            copy.wait()
        full = jnp.dot(left, held[k], preferred_element_type=F32).astype(BF16)
        for d in range(count):
            out[d, wide * k : wide * (k + 1), :] = full[:, width * d : width * (d + 1)]


def collect(pieces, half, scale, rows):
    count, _, width = pieces.shape
    rank = pieces.shape[1] // (2 * SEGS + 1)
    wide = SEGS * rank
    slot_at = lax.broadcasted_iota(jnp.int32, (rows // rank, 1, width), 0).astype(F32)
    total = jnp.zeros((rows // rank, rank, width), F32)
    for d in range(count):
        notes = pieces[d, 2 * wide :, :].astype(F32)
        for i in range(SEGS):
            slot = notes[half * SEGS + i : half * SEGS + i + 1]
            first = half * wide + rank * i
            piece = pieces[d, first : first + rank, :].astype(F32)
            total = total + jnp.where(slot_at == slot[None], piece[None], 0.0)
    return (scale * total).reshape(rows, width).astype(BF16)


def collect_kernel(pieces, down_out, up_out):
    down_out[...] = collect(pieces, 0, 1.0, down_out.shape[0])
    up_out[...] = collect(pieces, 1, ADAPTER_SCALE, up_out.shape[0])


def unpack_kernel(sums, down_out, up_out):
    count, rows, width = sums.shape
    for half, ref in enumerate((down_out, up_out)):
        _, slots, rank, _ = ref.shape
        for d in range(count):
            block = sums[d, half * (rows // 2) : (half + 1) * (rows // 2)]
            ref[0, :, :, width * d : width * (d + 1)] = block.reshape(slots, rank, width)


def hand_on_kernel(info, arrived, fwd, up, out):
    rows = out.shape[1]
    first = pl.multiple_of(pl.program_id(0) * rows, rows)
    starts, lives, slots = recall(info, 0)
    wide = spread(fwd[:, pl.ds(first, rows)], alive_rows(starts, lives, first, rows))
    update = lax.dot_general(
        wide, pick_rows(up, slots), (((0,), (0,)), ((), ())), preferred_element_type=F32
    )
    out[0] = (arrived[0].astype(F32) + ADAPTER_SCALE * update).astype(BF16)


def in_hbm(value):
    return pltpu.with_memory_space_constraint(value, pltpu.HBM)


def shift(value, steps):
    count = lax.axis_size("section")
    return lax.ppermute(value, "section", [(i, (i + steps) % count) for i in range(count)])


def exchange_add(value, distance):
    count = lax.axis_size("tensor")
    return value + lax.ppermute(value, "tensor", [(i, i ^ distance) for i in range(count)])


def per_device(
    act_inbox,
    grad_inbox,
    queries,
    keys_values,
    saved_attn,
    down_adapt,
    up_adapt,
    seg_blocks,
    seg_pads,
    seg_tenant,
    adapter_table,
):
    _, length, width = act_inbox.shape
    _, slot_count, rank, _ = up_adapt.shape
    wide = SEGS * rank
    scalars = (seg_blocks, seg_pads, seg_tenant, adapter_table)
    tensor_count, dp_count = lax.axis_size("tensor"), lax.axis_size("dp")
    part = width // dp_count
    piece = length * width * 2

    cuts = 1
    vmem = lambda shape: pltpu.VMEM(shape, BF16)
    ahead, info = pl.pallas_call(
        prepare_kernel,
        out_shape=(vmem((wide + rank, width)), jax.ShapeDtypeStruct((1, 2 * SEGS * SEGS), jnp.int32)),
        in_specs=[HBM] * 7,
        out_specs=(VMEM, SMEM),
        scratch_shapes=[
            pltpu.SMEM((3, *seg_blocks.shape), jnp.int32),
            pltpu.SMEM(adapter_table.shape, jnp.int32),
            pltpu.VMEM((length, width), BF16),
            pltpu.VMEM(down_adapt.shape, BF16),
            pltpu.VMEM(up_adapt.shape, BF16),
            pltpu.SemaphoreType.DMA((6 + cuts,)),
        ],
        compiler_params=PARAMS,
        cost_estimate=cost(2 * wide * length * width, 5 * piece),
        name="prepare",
    )(*[in_hbm(x) for x in (*scalars, saved_attn, down_adapt, up_adapt)])
    theirs = shift(ahead, 1)

    attention_cost = cost(
        2 * length * MOST_BLOCKS * BLOCK * width + wide * length * width,
        piece * 3 // 4,
        length * MOST_BLOCKS * BLOCK * width // HD // 2,
    )
    half = length // 2
    early = pl.pallas_call(
        early_attention_kernel,
        out_shape=pltpu.VMEM((rank, half), F32),
        in_specs=[SMEM] + [VMEM] * 3,
        out_specs=VMEM,
        scratch_shapes=[pltpu.VMEM((half, width), BF16)],
        compiler_params=PARAMS,
        cost_estimate=attention_cost,
        name="early_attention",
    )(info, queries, keys_values, down_adapt)
    theirs, early = lax.optimization_barrier((theirs, early))

    grad_part = pl.pallas_call(
        back_gradient_kernel,
        out_shape=vmem((rank, length)),
        in_specs=[VMEM] * 2,
        out_specs=VMEM,
        compiler_params=PARAMS,
        cost_estimate=cost(2 * wide * length * width, piece),
        name="back_gradient",
    )(theirs, grad_inbox)
    grad_part = shift(grad_part, -1)

    def copies(value, count):
        return jnp.broadcast_to(value[None], (count, *value.shape))

    parts = copies(jnp.concatenate([theirs[wide:, length : 2 * length], grad_part], axis=0), tensor_count)
    queries, act_inbox, parts = lax.optimization_barrier((queries, act_inbox, parts))
    arrived = shift(act_inbox, 1)
    parts = lax.all_to_all(parts, "tensor", 0, 0)

    late = pl.pallas_call(
        late_attention_kernel,
        out_shape=pltpu.VMEM((rank, half), F32),
        in_specs=[SMEM] + [VMEM] * 3,
        out_specs=VMEM,
        scratch_shapes=[pltpu.VMEM((half, width), BF16)],
        compiler_params=PARAMS,
        cost_estimate=attention_cost,
        name="late_attention",
    )(info, queries, keys_values, down_adapt)

    fwd_sum = exchange_add(jnp.concatenate([early, late], axis=1), 1)

    pieces = pl.pallas_call(
        contract_kernel,
        out_shape=jax.ShapeDtypeStruct((dp_count, 2 * wide + rank, part), BF16),
        in_specs=[SMEM, VMEM, VMEM, HBM, HBM],
        out_specs=VMEM,
        scratch_shapes=[
            pltpu.VMEM((2, length, width), BF16),
            pltpu.SemaphoreType.DMA((2, 4)),
        ],
        compiler_params=PARAMS,
        cost_estimate=cost(4 * wide * length * width, 2 * piece),
        name="contract",
    )(info, parts, theirs, in_hbm(saved_attn), in_hbm(grad_inbox))
    pieces, fwd_sum = lax.optimization_barrier((pieces, fwd_sum))
    fwd_sum = exchange_add(fwd_sum, 2)
    pieces = lax.all_to_all(pieces, "dp", 0, 0)
    pieces, fwd_sum = lax.optimization_barrier((pieces, fwd_sum))

    down_sum, up_sum = pl.pallas_call(
        collect_kernel,
        out_shape=(vmem((slot_count * rank, part)),) * 2,
        in_specs=[VMEM],
        out_specs=(VMEM, VMEM),
        compiler_params=PARAMS,
        cost_estimate=cost(4 * dp_count * SEGS * slot_count * rank * part, piece // 4),
        name="collect",
    )(pieces)
    up_sum = shift(up_sum, -1)
    sums = copies(jnp.concatenate([down_sum, up_sum], axis=0), dp_count)
    sums, arrived, fwd_sum = lax.optimization_barrier((sums, arrived, fwd_sum))
    fwd_sum = exchange_add(fwd_sum, 4)
    sums = lax.all_to_all(sums, "dp", 0, 0)

    rows = 128
    new_acts = pl.pallas_call(
        hand_on_kernel,
        grid=(length // rows,),
        out_shape=jax.ShapeDtypeStruct(act_inbox.shape, BF16),
        in_specs=[SMEM, pl.BlockSpec((1, rows, width), lambda i: (0, i, 0)), VMEM, VMEM],
        out_specs=pl.BlockSpec((1, rows, width), lambda i: (0, i, 0)),
        compiler_params=PARAMS,
        cost_estimate=cost(2 * wide * length * width, 2 * piece),
        name="hand_on",
    )(info, arrived, fwd_sum, up_adapt)

    sums, new_acts = lax.optimization_barrier((sums, new_acts))
    grad_down, grad_up = pl.pallas_call(
        unpack_kernel,
        out_shape=(jax.ShapeDtypeStruct(up_adapt.shape, BF16),) * 2,
        in_specs=[VMEM],
        out_specs=(VMEM, VMEM),
        compiler_params=PARAMS,
        cost_estimate=cost(0, piece),
        name="unpack",
    )(sums)
    return new_acts, grad_down, grad_up


def solution(mesh):
    placed = (
        P("section", "dp", "tensor"),
        P("section", "dp", "tensor"),
        P("section", "dp", "tensor"),
        P("section", None, "dp", "tensor"),
        P("section", "dp", "tensor"),
        P("section", None, None, "tensor"),
        P("section", None, None, "tensor"),
        P("section", None, "dp", None),
        P("section", None, "dp", None),
        P("section", None, "dp", None),
        P(),
    )
    return jax.shard_map(
        per_device,
        mesh=mesh,
        in_specs=placed,
        out_specs=(
            P("section", "dp", "tensor"),
            P("section", None, None, "tensor"),
            P("section", None, None, "tensor"),
        ),
        check_vma=False,
    )
```

```python
import math

import jax
import jax.numpy as jnp
from jax import lax
from jax.experimental import pallas as pl
from jax.experimental.pallas import tpu as pltpu
from jax.sharding import PartitionSpec as P

HD = 128
BLOCK = 64
SEGS = 3
MOST_BLOCKS = 4
ADAPTER_SCALE = 2.0
BF16 = jnp.bfloat16
F32 = jnp.float32
TENSOR = ("z4", "zi")
SMEM = pl.BlockSpec(memory_space=pltpu.SMEM)
VMEM = pl.BlockSpec(memory_space=pltpu.VMEM)
HBM = pl.BlockSpec(memory_space=pltpu.HBM)
PARAMS = pltpu.CompilerParams(vmem_limit_bytes=20 * 1024 * 1024)


def cost(flops, size, exps=0):
    return pl.CostEstimate(flops=flops, bytes_accessed=size, transcendentals=exps)


def rows_by_rows(left, right):
    return lax.dot_general(left, right, (((1,), (1,)), ((), ())), preferred_element_type=F32)


def segments(blocks, pads, tenants, table, batch):
    starts, lives, slots = [], [], []
    start = jnp.int32(0)
    for i in range(SEGS):
        end = start + blocks[0, batch, 0, i] * BLOCK
        starts.append(start)
        lives.append(end - pads[0, batch, 0, i])
        slots.append(table[tenants[0, batch, 0, i]])
        start = end
    return starts, lives, slots


def alive_rows(starts, lives, first, count):
    token = first + lax.broadcasted_iota(jnp.int32, (1, count), 1)
    return [(token >= s) & (token < e) for s, e in zip(starts, lives)]


def pick_rows(adapters, slots):
    return jnp.concatenate([adapters[0, s] for s in slots], axis=0)


def fold(full, masks, rank):
    return sum(jnp.where(m, full[rank * i : rank * (i + 1)], 0.0) for i, m in enumerate(masks))


def spread(ranked, masks):
    wide = ranked.astype(F32)
    return jnp.concatenate([jnp.where(m, wide, 0.0) for m in masks], axis=0).astype(BF16)


def prepare_kernel(blocks, pads, tenants, table, saved, down, up, out, info, raw, listed, held, downs, ups, sems):
    _, _, rank, width = up.shape
    length = saved.shape[1]
    wide = SEGS * rank
    first = [pltpu.make_async_copy(src, raw.at[i], sems.at[i]) for i, src in enumerate((blocks, pads, tenants))]
    first.append(pltpu.make_async_copy(table, listed, sems.at[3]))
    adapters = [
        pltpu.make_async_copy(up, ups, sems.at[4]),
        pltpu.make_async_copy(down, downs, sems.at[5]),
    ]
    tokens = pltpu.make_async_copy(saved.at[0], held, sems.at[6])
    for copy in first + [tokens] + adapters:
        copy.start()
    for copy in first:
        copy.wait()
    for batch in range(2):
        found = segments(raw.at[0], raw.at[1], raw.at[2], listed, batch)
        for i, values in enumerate(found):
            for k, value in enumerate(values):
                info[0, SEGS * (SEGS * batch + i) + k] = value
    starts, lives, slots = found
    masks = alive_rows(starts, lives, 0, length)
    row = lax.broadcasted_iota(jnp.int32, (rank, length), 0)
    notes = jnp.zeros((rank, length), F32)
    for i in range(SEGS):
        notes = jnp.where((row == i) & masks[i], 1.0, notes)
        notes = jnp.where(row == SEGS + i, slots[i].astype(F32), notes)
    out[wide:, :length] = notes.astype(BF16)
    out[wide:, 3 * length :] = jnp.zeros((rank, width - 3 * length), BF16)
    adapters[0].wait()
    for i in range(SEGS):
        out[rank * i : rank * (i + 1), :] = ups[0, slots[i]]
    adapters[1].wait()
    tokens.wait()
    ranks = fold(rows_by_rows(pick_rows(downs, slots), held[...]), masks, rank)
    high = ranks.astype(BF16)
    out[wide:, length : 2 * length] = high
    out[wide:, 2 * length : 3 * length] = (ranks - high.astype(F32)).astype(BF16)


def recall(info, batch):
    base = SEGS * SEGS * batch
    return [[info[0, base + SEGS * i + k] for k in range(SEGS)] for i in range(3)]


def note_masks(ahead, wide, length):
    notes = ahead[wide:, :length].astype(F32)
    return [notes[i : i + 1] > 0.5 for i in range(SEGS)]


def back_gradient_kernel(ahead, grads, out):
    rank, length = out.shape
    wide = SEGS * rank
    full = rows_by_rows(ahead[:wide, :], grads[0])
    out[...] = fold(full, note_masks(ahead, wide, length), rank)


def attend_blocks(info, queries, keys_values, attended, first, last, base):
    heads = queries.shape[2] // HD
    starts, lives, _ = recall(info, 0)
    power = math.log2(math.e) / math.sqrt(HD)
    for j in range(first, last):
        low, high = max(0, j + 1 - MOST_BLOCKS) * BLOCK, (j + 1) * BLOCK
        here = slice(j * BLOCK, high)
        start, live = starts[0], lives[0]
        for i in range(1, SEGS):
            inside = j * BLOCK >= starts[i]
            start = jnp.where(inside, starts[i], start)
            live = jnp.where(inside, lives[i], live)
        query_at = j * BLOCK + lax.broadcasted_iota(jnp.int32, (BLOCK, high - low), 0)
        key_at = low + lax.broadcasted_iota(jnp.int32, (BLOCK, high - low), 1)
        seen = ((key_at <= query_at) & (key_at >= start))[None]
        alive = (j * BLOCK + lax.broadcasted_iota(jnp.int32, (BLOCK, 1), 0) < live)[None]
        stacked = jnp.concatenate(
            [queries[0, here, HD * h : HD * (h + 1)] for h in range(heads)], axis=0
        )
        scores = rows_by_rows(stacked, keys_values[0, 0, low:high, :])
        scores = jnp.where(seen, scores.reshape(heads, BLOCK, high - low), -1e30)
        top = jnp.max(scores, axis=-1, keepdims=True)
        exponent = jnp.exp2((scores - top) * power)
        total = jnp.sum(exponent, axis=-1, keepdims=True)
        weights = (exponent * jnp.where(alive, 1.0 / total, 0.0)).astype(BF16)
        mixed = jnp.dot(
            weights.reshape(heads * BLOCK, high - low),
            keys_values[0, 1, low:high, :],
            preferred_element_type=F32,
        ).astype(BF16)
        for h in range(heads):
            at = slice((j - base) * BLOCK, (j + 1 - base) * BLOCK)
            attended[at, HD * h : HD * (h + 1)] = mixed[BLOCK * h : BLOCK * (h + 1)]


def ranked_attention(info, down, attended, first, out):
    rank, length = out.shape
    starts, lives, slots = recall(info, 0)
    full = rows_by_rows(pick_rows(down, slots), attended[...])
    out[...] = fold(full, alive_rows(starts, lives, first, length), rank)


def early_attention_kernel(info, queries, keys_values, down, out, attended):
    attend_blocks(info, queries, keys_values, attended, 0, attended.shape[0] // BLOCK, 0)
    ranked_attention(info, down, attended, 0, out)


def late_attention_kernel(info, queries, keys_values, down, out, attended):
    half = attended.shape[0] // BLOCK
    attend_blocks(info, queries, keys_values, attended, half, 2 * half, half)
    ranked_attention(info, down, attended, half * BLOCK, out)


def contract_kernel(info, parts, ahead, saved, grads, out, held, sems):
    _, rows, length = parts.shape
    rank = rows // 2
    wide = SEGS * rank
    cuts = sems.shape[1]
    tall = length // cuts
    copies = []
    for k, ref in enumerate((saved, grads)):
        for i in range(cuts):
            at = pl.ds(tall * i, tall)
            copies.append(pltpu.make_async_copy(ref.at[0, at], held.at[k, at], sems.at[k, i]))
    for copy in copies:
        copy.start()
    starts, lives, slots = recall(info, 1)
    total = jnp.sum(parts[...].astype(F32), axis=0)
    back_rank = total[:rank].astype(BF16)
    back_grad = (ADAPTER_SCALE * total[rank:]).astype(BF16)
    count, _, width = out.shape
    row = lax.broadcasted_iota(jnp.int32, (rank, width), 0)
    notes = ahead[wide:, :width].astype(F32)
    for i in range(SEGS):
        notes = jnp.where(row == i, slots[i].astype(F32), notes)
    lefts = (
        spread(back_grad, alive_rows(starts, lives, 0, length)),
        spread(back_rank, note_masks(ahead, wide, length)),
    )
    for d in range(count):
        out[d, 2 * wide :, :] = notes.astype(BF16)
    for k, left in enumerate(lefts):
        for copy in copies[cuts * k : cuts * (k + 1)]:
            copy.wait()
        full = jnp.dot(left, held[k], preferred_element_type=F32).astype(BF16)
        for d in range(count):
            out[d, wide * k : wide * (k + 1), :] = full[:, width * d : width * (d + 1)]


def collect(pieces, half, scale, rows):
    count, _, width = pieces.shape
    rank = pieces.shape[1] // (2 * SEGS + 1)
    wide = SEGS * rank
    slot_at = lax.broadcasted_iota(jnp.int32, (rows // rank, 1, width), 0).astype(F32)
    total = jnp.zeros((rows // rank, rank, width), F32)
    for d in range(count):
        notes = pieces[d, 2 * wide :, :].astype(F32)
        for i in range(SEGS):
            slot = notes[half * SEGS + i : half * SEGS + i + 1]
            first = half * wide + rank * i
            piece = pieces[d, first : first + rank, :].astype(F32)
            total = total + jnp.where(slot_at == slot[None], piece[None], 0.0)
    return (scale * total).reshape(rows, width).astype(BF16)


def collect_up_kernel(pieces, out):
    out[...] = collect(pieces, 1, ADAPTER_SCALE, out.shape[0])


def copy_to_all(block, out, first, sems):
    rows = block.shape[0]
    copies = [
        pltpu.make_async_copy(block, out.at[d, pl.ds(first, rows)], sems.at[d]) for d in range(out.shape[0])
    ]
    for copy in copies:
        copy.start()
    for copy in copies:
        copy.wait()


def collect_down_kernel(pieces, out, block, sems):
    block[...] = collect(pieces, 0, 1.0, block.shape[0])
    copy_to_all(block, out, 0, sems)


def add_up_kernel(block, half, out, sems):
    del half
    copy_to_all(block, out, block.shape[0], sems)


def unpack_kernel(sums, down_out, up_out):
    count, rows, width = sums.shape
    for half, ref in enumerate((down_out, up_out)):
        _, slots, rank, _ = ref.shape
        for d in range(count):
            block = sums[d, half * (rows // 2) : (half + 1) * (rows // 2)]
            ref[0, :, :, width * d : width * (d + 1)] = block.reshape(slots, rank, width)


def hand_on_kernel(info, arrived, fwd, up, out):
    rows = out.shape[1]
    first = pl.multiple_of(pl.program_id(0) * rows, rows)
    starts, lives, slots = recall(info, 0)
    wide = spread(fwd[:, pl.ds(first, rows)], alive_rows(starts, lives, first, rows))
    update = lax.dot_general(
        wide, pick_rows(up, slots), (((0,), (0,)), ((), ())), preferred_element_type=F32
    )
    out[0] = (arrived[0].astype(F32) + ADAPTER_SCALE * update).astype(BF16)


def in_hbm(value):
    return pltpu.with_memory_space_constraint(value, pltpu.HBM)


def shift(value, steps):
    count = lax.axis_size("section")
    return lax.ppermute(value, "section", [(i, (i + steps) % count) for i in range(count)])


def exchange_add(value, distance):
    count = lax.axis_size(TENSOR)
    return value + lax.ppermute(value, TENSOR, [(i, i ^ distance) for i in range(count)])


def per_device(
    act_inbox,
    grad_inbox,
    queries,
    keys_values,
    saved_attn,
    down_adapt,
    up_adapt,
    seg_blocks,
    seg_pads,
    seg_tenant,
    adapter_table,
):
    _, length, width = act_inbox.shape
    _, slot_count, rank, _ = up_adapt.shape
    wide = SEGS * rank
    scalars = (seg_blocks, seg_pads, seg_tenant, adapter_table)
    dp_count = lax.axis_size("dp")
    part = width // dp_count
    piece = length * width * 2

    vmem = lambda shape: pltpu.VMEM(shape, BF16)
    ahead, info = pl.pallas_call(
        prepare_kernel,
        out_shape=(vmem((wide + rank, width)), jax.ShapeDtypeStruct((1, 2 * SEGS * SEGS), jnp.int32)),
        in_specs=[HBM] * 7,
        out_specs=(VMEM, SMEM),
        scratch_shapes=[
            pltpu.SMEM((3, *seg_blocks.shape), jnp.int32),
            pltpu.SMEM(adapter_table.shape, jnp.int32),
            pltpu.VMEM((length, width), BF16),
            pltpu.VMEM(down_adapt.shape, BF16),
            pltpu.VMEM(up_adapt.shape, BF16),
            pltpu.SemaphoreType.DMA((7,)),
        ],
        compiler_params=PARAMS,
        cost_estimate=cost(2 * wide * length * width, 5 * piece),
        name="prepare",
    )(*[in_hbm(x) for x in (*scalars, saved_attn, down_adapt, up_adapt)])
    theirs = shift(ahead, 1)

    attention_cost = cost(
        2 * length * MOST_BLOCKS * BLOCK * width + wide * length * width,
        piece * 3 // 4,
        length * MOST_BLOCKS * BLOCK * width // HD // 2,
    )
    half = length // 2
    early = pl.pallas_call(
        early_attention_kernel,
        out_shape=pltpu.VMEM((rank, half), F32),
        in_specs=[SMEM] + [VMEM] * 3,
        out_specs=VMEM,
        scratch_shapes=[pltpu.VMEM((half, width), BF16)],
        compiler_params=PARAMS,
        cost_estimate=attention_cost,
        name="early_attention",
    )(info, queries, keys_values, down_adapt)
    theirs, early = lax.optimization_barrier((theirs, early))

    grad_part = pl.pallas_call(
        back_gradient_kernel,
        out_shape=pltpu.VMEM((rank, length), F32),
        in_specs=[VMEM] * 2,
        out_specs=VMEM,
        compiler_params=PARAMS,
        cost_estimate=cost(2 * wide * length * width, piece),
        name="back_gradient",
    )(theirs, grad_inbox)
    grad_part = shift(grad_part, -1)

    def copies(value, count):
        return jnp.broadcast_to(value[None], (count, *value.shape))

    back = theirs[wide:, length : 2 * length].astype(F32) + theirs[wide:, 2 * length : 3 * length].astype(F32)
    parts = jnp.concatenate([back, grad_part], axis=0)
    queries, act_inbox, parts = lax.optimization_barrier((queries, act_inbox, parts))
    parts = exchange_add(parts, 4).astype(BF16)
    arrived = shift(act_inbox, 1)
    late = pl.pallas_call(
        late_attention_kernel,
        out_shape=pltpu.VMEM((rank, half), F32),
        in_specs=[SMEM] + [VMEM] * 3,
        out_specs=VMEM,
        scratch_shapes=[pltpu.VMEM((half, width), BF16)],
        compiler_params=PARAMS,
        cost_estimate=attention_cost,
        name="late_attention",
    )(info, queries, keys_values, down_adapt)
    parts, late = lax.optimization_barrier((parts, late))
    parts = lax.all_to_all(copies(parts, lax.axis_size("zi")), "zi", 0, 0)

    fwd_sum = exchange_add(jnp.concatenate([early, late], axis=1), 1)

    pieces = pl.pallas_call(
        contract_kernel,
        out_shape=jax.ShapeDtypeStruct((dp_count, 2 * wide + rank, part), BF16),
        in_specs=[SMEM, VMEM, VMEM, HBM, HBM],
        out_specs=VMEM,
        scratch_shapes=[
            pltpu.VMEM((2, length, width), BF16),
            pltpu.SemaphoreType.DMA((2, 4)),
        ],
        compiler_params=PARAMS,
        cost_estimate=cost(4 * wide * length * width, 2 * piece),
        name="contract",
    )(info, parts, theirs, in_hbm(saved_attn), in_hbm(grad_inbox))
    pieces, fwd_sum = lax.optimization_barrier((pieces, fwd_sum))
    fwd_sum = exchange_add(fwd_sum, 2)
    pieces = lax.all_to_all(pieces, "dp", 0, 0)
    pieces, fwd_sum = lax.optimization_barrier((pieces, fwd_sum))

    rows = slot_count * rank
    up_sum = pl.pallas_call(
        collect_up_kernel,
        out_shape=vmem((rows, part)),
        in_specs=[VMEM],
        out_specs=VMEM,
        compiler_params=PARAMS,
        cost_estimate=cost(2 * dp_count * SEGS * rows * part, piece // 4),
        name="collect_up",
    )(pieces)
    pieces, up_sum = lax.optimization_barrier((pieces, up_sum))
    sums_shape = jax.ShapeDtypeStruct((dp_count, 2 * rows, part), BF16)
    sums = pl.pallas_call(
        collect_down_kernel,
        out_shape=sums_shape,
        in_specs=[VMEM],
        out_specs=HBM,
        scratch_shapes=[pltpu.VMEM((rows, part), BF16), pltpu.SemaphoreType.DMA((dp_count,))],
        compiler_params=PARAMS,
        cost_estimate=cost(2 * dp_count * SEGS * rows * part, piece // 2),
        name="collect_down",
    )(pieces)
    sums = pl.pallas_call(
        add_up_kernel,
        out_shape=sums_shape,
        in_specs=[VMEM, HBM],
        out_specs=HBM,
        scratch_shapes=[pltpu.SemaphoreType.DMA((dp_count,))],
        input_output_aliases={1: 0},
        compiler_params=PARAMS,
        cost_estimate=cost(0, piece // 4),
        name="add_up",
    )(shift(up_sum, -1), sums)
    sums, arrived, fwd_sum = lax.optimization_barrier((sums, arrived, fwd_sum))
    fwd_sum = exchange_add(fwd_sum, 4)
    sums = lax.all_to_all(sums, "dp", 0, 0)

    rows = 128
    new_acts = pl.pallas_call(
        hand_on_kernel,
        grid=(length // rows,),
        out_shape=jax.ShapeDtypeStruct(act_inbox.shape, BF16),
        in_specs=[SMEM, pl.BlockSpec((1, rows, width), lambda i: (0, i, 0)), VMEM, VMEM],
        out_specs=pl.BlockSpec((1, rows, width), lambda i: (0, i, 0)),
        compiler_params=PARAMS,
        cost_estimate=cost(2 * wide * length * width, 2 * piece),
        name="hand_on",
    )(info, arrived, fwd_sum, up_adapt)

    sums, new_acts = lax.optimization_barrier((sums, new_acts))
    grad_down, grad_up = pl.pallas_call(
        unpack_kernel,
        out_shape=(jax.ShapeDtypeStruct(up_adapt.shape, BF16),) * 2,
        in_specs=[VMEM],
        out_specs=(VMEM, VMEM),
        compiler_params=PARAMS,
        cost_estimate=cost(0, piece),
        name="unpack",
    )(sums)
    return new_acts, grad_down, grad_up


def solution(mesh):
    section, tensor, dp = (mesh.shape[name] for name in ("section", "tensor", "dp"))
    fine = jax.sharding.Mesh(mesh.devices.reshape(section, 2, tensor // 2, dp), ("section", *TENSOR, "dp"))
    rows = P("section", "dp", TENSOR)
    adapters = P("section", None, None, TENSOR)
    scalars = P("section", None, "dp", None)
    return jax.shard_map(
        per_device,
        mesh=fine,
        in_specs=(
            rows,
            rows,
            rows,
            P("section", None, "dp", TENSOR),
            rows,
            adapters,
            adapters,
            scalars,
            scalars,
            scalars,
            P(),
        ),
        out_specs=(rows, adapters, adapters),
        check_vma=False,
    )
```

```python
import math

import jax
import jax.numpy as jnp
from jax import lax
from jax.experimental import pallas as pl
from jax.experimental.pallas import tpu as pltpu
from jax.sharding import PartitionSpec as P

HD = 128
BLOCK = 64
SEGS = 3
MOST_BLOCKS = 4
ADAPTER_SCALE = 2.0
BF16 = jnp.bfloat16
F32 = jnp.float32
TENSOR = ("z4", "zi")
SMEM = pl.BlockSpec(memory_space=pltpu.SMEM)
VMEM = pl.BlockSpec(memory_space=pltpu.VMEM)
HBM = pl.BlockSpec(memory_space=pltpu.HBM)
PARAMS = pltpu.CompilerParams(vmem_limit_bytes=20 * 1024 * 1024)


def cost(flops, size, exps=0):
    return pl.CostEstimate(flops=flops, bytes_accessed=size, transcendentals=exps)


def rows_by_rows(left, right):
    return lax.dot_general(left, right, (((1,), (1,)), ((), ())), preferred_element_type=F32)


def segments(blocks, pads, tenants, table, batch):
    starts, lives, slots = [], [], []
    start = jnp.int32(0)
    for i in range(SEGS):
        end = start + blocks[0, batch, 0, i] * BLOCK
        starts.append(start)
        lives.append(end - pads[0, batch, 0, i])
        slots.append(table[tenants[0, batch, 0, i]])
        start = end
    return starts, lives, slots


def alive_rows(starts, lives, first, count):
    token = first + lax.broadcasted_iota(jnp.int32, (1, count), 1)
    return [(token >= s) & (token < e) for s, e in zip(starts, lives)]


def pick_rows(adapters, slots):
    return jnp.concatenate([adapters[0, s] for s in slots], axis=0)


def fold(full, masks, rank):
    return sum(jnp.where(m, full[rank * i : rank * (i + 1)], 0.0) for i, m in enumerate(masks))


def spread(ranked, masks):
    wide = ranked.astype(F32)
    return jnp.concatenate([jnp.where(m, wide, 0.0) for m in masks], axis=0).astype(BF16)


def prepare_kernel(blocks, pads, tenants, table, saved, down, up, out, info, raw, listed, held, downs, ups, sems):
    _, _, rank, width = up.shape
    length = saved.shape[1]
    wide = SEGS * rank
    first = [pltpu.make_async_copy(src, raw.at[i], sems.at[i]) for i, src in enumerate((blocks, pads, tenants))]
    first.append(pltpu.make_async_copy(table, listed, sems.at[3]))
    adapters = [
        pltpu.make_async_copy(up, ups, sems.at[4]),
        pltpu.make_async_copy(down, downs, sems.at[5]),
    ]
    tokens = pltpu.make_async_copy(saved.at[0], held, sems.at[6])
    for copy in first + [tokens] + adapters:
        copy.start()
    for copy in first:
        copy.wait()
    for batch in range(2):
        found = segments(raw.at[0], raw.at[1], raw.at[2], listed, batch)
        for i, values in enumerate(found):
            for k, value in enumerate(values):
                info[0, SEGS * (SEGS * batch + i) + k] = value
    starts, lives, slots = found
    masks = alive_rows(starts, lives, 0, length)
    row = lax.broadcasted_iota(jnp.int32, (rank, length), 0)
    notes = jnp.zeros((rank, length), F32)
    for i in range(SEGS):
        notes = jnp.where((row == i) & masks[i], 1.0, notes)
        notes = jnp.where(row == SEGS + i, slots[i].astype(F32), notes)
    out[wide:, :length] = notes.astype(BF16)
    out[wide:, 3 * length :] = jnp.zeros((rank, width - 3 * length), BF16)
    adapters[0].wait()
    for i in range(SEGS):
        out[rank * i : rank * (i + 1), :] = ups[0, slots[i]]
    adapters[1].wait()
    tokens.wait()
    ranks = fold(rows_by_rows(pick_rows(downs, slots), held[...]), masks, rank)
    high = ranks.astype(BF16)
    out[wide:, length : 2 * length] = high
    out[wide:, 2 * length : 3 * length] = (ranks - high.astype(F32)).astype(BF16)


def recall(info, batch):
    base = SEGS * SEGS * batch
    return [[info[0, base + SEGS * i + k] for k in range(SEGS)] for i in range(3)]


def note_masks(ahead, wide, length):
    notes = ahead[wide:, :length].astype(F32)
    return [notes[i : i + 1] > 0.5 for i in range(SEGS)]


def back_gradient_kernel(ahead, grads, out):
    rank, length = out.shape
    wide = SEGS * rank
    full = rows_by_rows(ahead[:wide, :], grads[0])
    out[...] = fold(full, note_masks(ahead, wide, length), rank)


def attend_blocks(info, queries, keys_values, attended):
    heads = queries.shape[2] // HD
    starts, lives, _ = recall(info, 0)
    power = math.log2(math.e) / math.sqrt(HD)
    for j in range(attended.shape[0] // BLOCK):
        low, high = max(0, j + 1 - MOST_BLOCKS) * BLOCK, (j + 1) * BLOCK
        here = slice(j * BLOCK, high)
        start, live = starts[0], lives[0]
        for i in range(1, SEGS):
            inside = j * BLOCK >= starts[i]
            start = jnp.where(inside, starts[i], start)
            live = jnp.where(inside, lives[i], live)
        query_at = j * BLOCK + lax.broadcasted_iota(jnp.int32, (BLOCK, high - low), 0)
        key_at = low + lax.broadcasted_iota(jnp.int32, (BLOCK, high - low), 1)
        seen = ((key_at <= query_at) & (key_at >= start))[None]
        alive = (j * BLOCK + lax.broadcasted_iota(jnp.int32, (BLOCK, 1), 0) < live)[None]
        stacked = jnp.concatenate(
            [queries[0, here, HD * h : HD * (h + 1)] for h in range(heads)], axis=0
        )
        scores = rows_by_rows(stacked, keys_values[0, 0, low:high, :])
        scores = jnp.where(seen, scores.reshape(heads, BLOCK, high - low), -1e30)
        top = jnp.max(scores, axis=-1, keepdims=True)
        exponent = jnp.exp2((scores - top) * power).astype(BF16)
        values = jnp.concatenate(
            [keys_values[0, 1, low:high, :], jnp.ones((high - low, HD), BF16)], axis=1
        )
        mixed = jnp.dot(
            exponent.reshape(heads * BLOCK, high - low), values, preferred_element_type=F32
        ).reshape(heads, BLOCK, 2 * HD)
        mixed = mixed[:, :, :HD] * jnp.where(alive, 1.0 / mixed[:, :, HD:], 0.0)
        mixed = mixed.astype(BF16).reshape(heads * BLOCK, HD)
        for h in range(heads):
            attended[here, HD * h : HD * (h + 1)] = mixed[BLOCK * h : BLOCK * (h + 1)]


def attention_kernel(info, queries, keys_values, down, out, attended):
    attend_blocks(info, queries, keys_values, attended)
    rank, length = out.shape
    starts, lives, slots = recall(info, 0)
    full = rows_by_rows(pick_rows(down, slots), attended[...])
    out[...] = fold(full, alive_rows(starts, lives, 0, length), rank)


def contract_kernel(info, parts, ahead, saved, grads, out, held, sems):
    _, rows, length = parts.shape
    rank = rows // 2
    wide = SEGS * rank
    cuts = sems.shape[1]
    tall = length // cuts
    copies = []
    for k, ref in enumerate((saved, grads)):
        for i in range(cuts):
            at = pl.ds(tall * i, tall)
            copies.append(pltpu.make_async_copy(ref.at[0, at], held.at[k, at], sems.at[k, i]))
    for copy in copies:
        copy.start()
    starts, lives, slots = recall(info, 1)
    total = jnp.sum(parts[...].astype(F32), axis=0)
    back_rank = total[:rank].astype(BF16)
    back_grad = (ADAPTER_SCALE * total[rank:]).astype(BF16)
    count, _, width = out.shape
    row = lax.broadcasted_iota(jnp.int32, (rank, width), 0)
    notes = ahead[wide:, :width].astype(F32)
    for i in range(SEGS):
        notes = jnp.where(row == i, slots[i].astype(F32), notes)
    lefts = (
        spread(back_grad, alive_rows(starts, lives, 0, length)),
        spread(back_rank, note_masks(ahead, wide, length)),
    )
    for d in range(count):
        out[d, 2 * wide :, :] = notes.astype(BF16)
    for k, left in enumerate(lefts):
        for copy in copies[cuts * k : cuts * (k + 1)]:
            copy.wait()
        full = jnp.dot(left, held[k], preferred_element_type=F32).astype(BF16)
        for d in range(count):
            out[d, wide * k : wide * (k + 1), :] = full[:, width * d : width * (d + 1)]


def collect(pieces, half, scale, rows):
    count, _, width = pieces.shape
    rank = pieces.shape[1] // (2 * SEGS + 1)
    wide = SEGS * rank
    slot_at = lax.broadcasted_iota(jnp.int32, (rows // rank, 1, width), 0).astype(F32)
    total = jnp.zeros((rows // rank, rank, width), F32)
    for d in range(count):
        notes = pieces[d, 2 * wide :, :].astype(F32)
        for i in range(SEGS):
            slot = notes[half * SEGS + i : half * SEGS + i + 1]
            first = half * wide + rank * i
            piece = pieces[d, first : first + rank, :].astype(F32)
            total = total + jnp.where(slot_at == slot[None], piece[None], 0.0)
    return (scale * total).reshape(rows, width).astype(BF16)


def collect_up_kernel(pieces, out):
    out[...] = collect(pieces, 1, ADAPTER_SCALE, out.shape[0])


def copy_to_all(block, out, first, sems):
    rows = block.shape[0]
    copies = [
        pltpu.make_async_copy(block, out.at[d, pl.ds(first, rows)], sems.at[d]) for d in range(out.shape[0])
    ]
    for copy in copies:
        copy.start()
    for copy in copies:
        copy.wait()


def collect_down_kernel(pieces, out, block, sems):
    block[...] = collect(pieces, 0, 1.0, block.shape[0])
    copy_to_all(block, out, 0, sems)


def add_up_kernel(block, half, out, sems):
    del half
    copy_to_all(block, out, block.shape[0], sems)


def unpack_kernel(sums, down_out, up_out):
    count, rows, width = sums.shape
    for half, ref in enumerate((down_out, up_out)):
        _, slots, rank, _ = ref.shape
        for d in range(count):
            block = sums[d, half * (rows // 2) : (half + 1) * (rows // 2)]
            ref[0, :, :, width * d : width * (d + 1)] = block.reshape(slots, rank, width)


def hand_on_kernel(info, arrived, fwd, up, out):
    rows = out.shape[1]
    first = pl.multiple_of(pl.program_id(0) * rows, rows)
    starts, lives, slots = recall(info, 0)
    wide = spread(fwd[:, pl.ds(first, rows)], alive_rows(starts, lives, first, rows))
    update = lax.dot_general(
        wide, pick_rows(up, slots), (((0,), (0,)), ((), ())), preferred_element_type=F32
    )
    out[0] = (arrived[0].astype(F32) + ADAPTER_SCALE * update).astype(BF16)


def in_hbm(value):
    return pltpu.with_memory_space_constraint(value, pltpu.HBM)


def shift(value, steps):
    count = lax.axis_size("section")
    return lax.ppermute(value, "section", [(i, (i + steps) % count) for i in range(count)])


def exchange_add(value, distance):
    count = lax.axis_size(TENSOR)
    return value + lax.ppermute(value, TENSOR, [(i, i ^ distance) for i in range(count)])


def per_device(
    act_inbox,
    grad_inbox,
    queries,
    keys_values,
    saved_attn,
    down_adapt,
    up_adapt,
    seg_blocks,
    seg_pads,
    seg_tenant,
    adapter_table,
):
    _, length, width = act_inbox.shape
    _, slot_count, rank, _ = up_adapt.shape
    wide = SEGS * rank
    scalars = (seg_blocks, seg_pads, seg_tenant, adapter_table)
    dp_count = lax.axis_size("dp")
    part = width // dp_count
    piece = length * width * 2

    vmem = lambda shape: pltpu.VMEM(shape, BF16)
    ahead, info = pl.pallas_call(
        prepare_kernel,
        out_shape=(vmem((wide + rank, width)), jax.ShapeDtypeStruct((1, 2 * SEGS * SEGS), jnp.int32)),
        in_specs=[HBM] * 7,
        out_specs=(VMEM, SMEM),
        scratch_shapes=[
            pltpu.SMEM((3, *seg_blocks.shape), jnp.int32),
            pltpu.SMEM(adapter_table.shape, jnp.int32),
            pltpu.VMEM((length, width), BF16),
            pltpu.VMEM(down_adapt.shape, BF16),
            pltpu.VMEM(up_adapt.shape, BF16),
            pltpu.SemaphoreType.DMA((7,)),
        ],
        compiler_params=PARAMS,
        cost_estimate=cost(2 * wide * length * width, 5 * piece),
        name="prepare",
    )(*[in_hbm(x) for x in (*scalars, saved_attn, down_adapt, up_adapt)])
    theirs = shift(ahead, 1)

    fwd_sum = pl.pallas_call(
        attention_kernel,
        out_shape=pltpu.VMEM((rank, length), F32),
        in_specs=[SMEM] + [VMEM] * 3,
        out_specs=VMEM,
        scratch_shapes=[pltpu.VMEM((length, width), BF16)],
        compiler_params=PARAMS,
        cost_estimate=cost(
            4 * length * MOST_BLOCKS * BLOCK * width + 2 * wide * length * width,
            piece * 3 // 2,
            length * MOST_BLOCKS * BLOCK * width // HD,
        ),
        name="attention",
    )(info, queries, keys_values, down_adapt)
    theirs, fwd_sum = lax.optimization_barrier((theirs, fwd_sum))

    grad_part = pl.pallas_call(
        back_gradient_kernel,
        out_shape=pltpu.VMEM((rank, length), F32),
        in_specs=[VMEM] * 2,
        out_specs=VMEM,
        compiler_params=PARAMS,
        cost_estimate=cost(2 * wide * length * width, piece),
        name="back_gradient",
    )(theirs, grad_inbox)
    grad_part = shift(grad_part, -1)

    def copies(value, count):
        return jnp.broadcast_to(value[None], (count, *value.shape))

    back = theirs[wide:, length : 2 * length].astype(F32) + theirs[wide:, 2 * length : 3 * length].astype(F32)
    parts = jnp.concatenate([back, grad_part], axis=0)
    act_inbox, fwd_sum, parts = lax.optimization_barrier((act_inbox, fwd_sum, parts))
    parts = exchange_add(parts, 4).astype(BF16)
    arrived = shift(act_inbox, 1)
    parts, fwd_sum = lax.optimization_barrier((parts, fwd_sum))
    parts = lax.all_to_all(copies(parts, lax.axis_size("zi")), "zi", 0, 0)
    fwd_sum = exchange_add(fwd_sum, 1)

    pieces = pl.pallas_call(
        contract_kernel,
        out_shape=jax.ShapeDtypeStruct((dp_count, 2 * wide + rank, part), BF16),
        in_specs=[SMEM, VMEM, VMEM, HBM, HBM],
        out_specs=VMEM,
        scratch_shapes=[
            pltpu.VMEM((2, length, width), BF16),
            pltpu.SemaphoreType.DMA((2, 4)),
        ],
        compiler_params=PARAMS,
        cost_estimate=cost(4 * wide * length * width, 2 * piece),
        name="contract",
    )(info, parts, theirs, in_hbm(saved_attn), in_hbm(grad_inbox))
    pieces, fwd_sum = lax.optimization_barrier((pieces, fwd_sum))
    pieces = lax.all_to_all(pieces, "dp", 0, 0)
    fwd_sum = exchange_add(fwd_sum, 2)
    pieces, fwd_sum = lax.optimization_barrier((pieces, fwd_sum))

    rows = slot_count * rank
    up_sum = pl.pallas_call(
        collect_up_kernel,
        out_shape=vmem((rows, part)),
        in_specs=[VMEM],
        out_specs=VMEM,
        compiler_params=PARAMS,
        cost_estimate=cost(2 * dp_count * SEGS * rows * part, piece // 4),
        name="collect_up",
    )(pieces)
    pieces, up_sum = lax.optimization_barrier((pieces, up_sum))
    sums_shape = jax.ShapeDtypeStruct((dp_count, 2 * rows, part), BF16)
    sums = pl.pallas_call(
        collect_down_kernel,
        out_shape=sums_shape,
        in_specs=[VMEM],
        out_specs=HBM,
        scratch_shapes=[pltpu.VMEM((rows, part), BF16), pltpu.SemaphoreType.DMA((dp_count,))],
        compiler_params=PARAMS,
        cost_estimate=cost(2 * dp_count * SEGS * rows * part, piece // 2),
        name="collect_down",
    )(pieces)
    sums = pl.pallas_call(
        add_up_kernel,
        out_shape=sums_shape,
        in_specs=[VMEM, HBM],
        out_specs=HBM,
        scratch_shapes=[pltpu.SemaphoreType.DMA((dp_count,))],
        input_output_aliases={1: 0},
        compiler_params=PARAMS,
        cost_estimate=cost(0, piece // 4),
        name="add_up",
    )(shift(up_sum, -1), sums)
    sums, arrived, fwd_sum = lax.optimization_barrier((sums, arrived, fwd_sum))
    fwd_sum = exchange_add(fwd_sum, 4)
    sums = lax.all_to_all(sums, "dp", 0, 0)

    rows = 128
    new_acts = pl.pallas_call(
        hand_on_kernel,
        grid=(length // rows,),
        out_shape=jax.ShapeDtypeStruct(act_inbox.shape, BF16),
        in_specs=[SMEM, pl.BlockSpec((1, rows, width), lambda i: (0, i, 0)), VMEM, VMEM],
        out_specs=pl.BlockSpec((1, rows, width), lambda i: (0, i, 0)),
        compiler_params=PARAMS,
        cost_estimate=cost(2 * wide * length * width, 2 * piece),
        name="hand_on",
    )(info, arrived, fwd_sum, up_adapt)

    sums, new_acts = lax.optimization_barrier((sums, new_acts))
    grad_down, grad_up = pl.pallas_call(
        unpack_kernel,
        out_shape=(jax.ShapeDtypeStruct(up_adapt.shape, BF16),) * 2,
        in_specs=[VMEM],
        out_specs=(VMEM, VMEM),
        compiler_params=PARAMS,
        cost_estimate=cost(0, piece),
        name="unpack",
    )(sums)
    return new_acts, grad_down, grad_up


def solution(mesh):
    section, tensor, dp = (mesh.shape[name] for name in ("section", "tensor", "dp"))
    fine = jax.sharding.Mesh(mesh.devices.reshape(section, 2, tensor // 2, dp), ("section", *TENSOR, "dp"))
    rows = P("section", "dp", TENSOR)
    adapters = P("section", None, None, TENSOR)
    scalars = P("section", None, "dp", None)
    return jax.shard_map(
        per_device,
        mesh=fine,
        in_specs=(
            rows,
            rows,
            rows,
            P("section", None, "dp", TENSOR),
            rows,
            adapters,
            adapters,
            scalars,
            scalars,
            scalars,
            P(),
        ),
        out_specs=(rows, adapters, adapters),
        check_vma=False,
    )
```

```python
import math

import jax
import jax.numpy as jnp
from jax import lax
from jax.experimental import pallas as pl
from jax.experimental.pallas import tpu as pltpu
from jax.sharding import PartitionSpec as P

HD = 128
BLOCK = 64
SEGS = 3
MOST_BLOCKS = 4
ADAPTER_SCALE = 2.0
BF16 = jnp.bfloat16
F32 = jnp.float32
TENSOR = ("z4", "zi")
SMEM = pl.BlockSpec(memory_space=pltpu.SMEM)
VMEM = pl.BlockSpec(memory_space=pltpu.VMEM)
HBM = pl.BlockSpec(memory_space=pltpu.HBM)
PARAMS = pltpu.CompilerParams(vmem_limit_bytes=20 * 1024 * 1024)


def cost(flops, size, exps=0):
    return pl.CostEstimate(flops=flops, bytes_accessed=size, transcendentals=exps)


def rows_by_rows(left, right):
    return lax.dot_general(left, right, (((1,), (1,)), ((), ())), preferred_element_type=F32)


def segments(blocks, pads, tenants, table, batch):
    starts, lives, slots = [], [], []
    start = jnp.int32(0)
    for i in range(SEGS):
        end = start + blocks[0, batch, 0, i] * BLOCK
        starts.append(start)
        lives.append(end - pads[0, batch, 0, i])
        slots.append(table[tenants[0, batch, 0, i]])
        start = end
    return starts, lives, slots


def alive_rows(starts, lives, first, count):
    token = first + lax.broadcasted_iota(jnp.int32, (1, count), 1)
    return [(token >= s) & (token < e) for s, e in zip(starts, lives)]


def pick_rows(adapters, slots):
    return jnp.concatenate([adapters[0, s] for s in slots], axis=0)


def fold(full, masks, rank):
    return sum(jnp.where(m, full[rank * i : rank * (i + 1)], 0.0) for i, m in enumerate(masks))


def spread(ranked, masks):
    wide = ranked.astype(F32)
    return jnp.concatenate([jnp.where(m, wide, 0.0) for m in masks], axis=0).astype(BF16)


def prepare_kernel(blocks, pads, tenants, table, saved, down, up, out, info, raw, listed, held, downs, ups, sems):
    _, _, rank, width = up.shape
    length = saved.shape[1]
    wide = SEGS * rank
    first = [pltpu.make_async_copy(src, raw.at[i], sems.at[i]) for i, src in enumerate((blocks, pads, tenants))]
    first.append(pltpu.make_async_copy(table, listed, sems.at[3]))
    adapters = [
        pltpu.make_async_copy(up, ups, sems.at[4]),
        pltpu.make_async_copy(down, downs, sems.at[5]),
    ]
    tokens = pltpu.make_async_copy(saved.at[0], held, sems.at[6])
    for copy in first + [tokens] + adapters:
        copy.start()
    for copy in first:
        copy.wait()
    for batch in range(2):
        found = segments(raw.at[0], raw.at[1], raw.at[2], listed, batch)
        for i, values in enumerate(found):
            for k, value in enumerate(values):
                info[0, SEGS * (SEGS * batch + i) + k] = value
    starts, lives, slots = found
    masks = alive_rows(starts, lives, 0, length)
    row = lax.broadcasted_iota(jnp.int32, (rank, length), 0)
    notes = jnp.zeros((rank, length), F32)
    for i in range(SEGS):
        notes = jnp.where((row == i) & masks[i], 1.0, notes)
        notes = jnp.where(row == SEGS + i, slots[i].astype(F32), notes)
    out[wide:, :length] = notes.astype(BF16)
    out[wide:, 3 * length :] = jnp.zeros((rank, width - 3 * length), BF16)
    adapters[0].wait()
    for i in range(SEGS):
        out[rank * i : rank * (i + 1), :] = ups[0, slots[i]]
    adapters[1].wait()
    tokens.wait()
    ranks = fold(rows_by_rows(pick_rows(downs, slots), held[...]), masks, rank)
    high = ranks.astype(BF16)
    out[wide:, length : 2 * length] = high
    out[wide:, 2 * length : 3 * length] = (ranks - high.astype(F32)).astype(BF16)


def recall(info, batch):
    base = SEGS * SEGS * batch
    return [[info[0, base + SEGS * i + k] for k in range(SEGS)] for i in range(3)]


def note_masks(ahead, wide, length):
    notes = ahead[wide:, :length].astype(F32)
    return [notes[i : i + 1] > 0.5 for i in range(SEGS)]


def back_gradient_kernel(ahead, grads, out):
    rank, length = out.shape
    wide = SEGS * rank
    full = rows_by_rows(ahead[:wide, :], grads[0])
    out[...] = fold(full, note_masks(ahead, wide, length), rank)


def attend_blocks(info, queries, keys_values, attended, first, last, base):
    heads = queries.shape[2] // HD
    starts, lives, _ = recall(info, 0)
    power = math.log2(math.e) / math.sqrt(HD)
    for j in range(first, last):
        low, high = max(0, j + 1 - MOST_BLOCKS) * BLOCK, (j + 1) * BLOCK
        here = slice(j * BLOCK, high)
        start, live = starts[0], lives[0]
        for i in range(1, SEGS):
            inside = j * BLOCK >= starts[i]
            start = jnp.where(inside, starts[i], start)
            live = jnp.where(inside, lives[i], live)
        query_at = j * BLOCK + lax.broadcasted_iota(jnp.int32, (BLOCK, high - low), 0)
        key_at = low + lax.broadcasted_iota(jnp.int32, (BLOCK, high - low), 1)
        seen = ((key_at <= query_at) & (key_at >= start))[None]
        alive = (j * BLOCK + lax.broadcasted_iota(jnp.int32, (BLOCK, 1), 0) < live)[None]
        stacked = jnp.concatenate(
            [queries[0, here, HD * h : HD * (h + 1)] for h in range(heads)], axis=0
        )
        scores = rows_by_rows(stacked, keys_values[0, 0, low:high, :])
        scores = jnp.where(seen, scores.reshape(heads, BLOCK, high - low), -1e30)
        top = jnp.max(scores, axis=-1, keepdims=True)
        exponent = jnp.exp2((scores - top) * power)
        total = jnp.sum(exponent, axis=-1, keepdims=True)
        weights = (exponent * jnp.where(alive, 1.0 / total, 0.0)).astype(BF16)
        mixed = jnp.dot(
            weights.reshape(heads * BLOCK, high - low),
            keys_values[0, 1, low:high, :],
            preferred_element_type=F32,
        ).astype(BF16)
        for h in range(heads):
            at = slice((j - base) * BLOCK, (j + 1 - base) * BLOCK)
            attended[at, HD * h : HD * (h + 1)] = mixed[BLOCK * h : BLOCK * (h + 1)]


def ranked_attention(info, down, attended, first, out):
    rank, length = out.shape
    starts, lives, slots = recall(info, 0)
    full = rows_by_rows(pick_rows(down, slots), attended[...])
    out[...] = fold(full, alive_rows(starts, lives, first, length), rank)


def early_attention_kernel(info, queries, keys_values, down, out, attended):
    attend_blocks(info, queries, keys_values, attended, 0, attended.shape[0] // BLOCK, 0)
    ranked_attention(info, down, attended, 0, out)


def late_attention_kernel(info, queries, keys_values, down, out, attended):
    half = attended.shape[0] // BLOCK
    attend_blocks(info, queries, keys_values, attended, half, 2 * half, half)
    ranked_attention(info, down, attended, half * BLOCK, out)


def contract_kernel(info, parts, ahead, saved, grads, out, held, sems):
    _, rows, length = parts.shape
    rank = rows // 2
    wide = SEGS * rank
    cuts = sems.shape[1]
    tall = length // cuts
    copies = []
    for k, ref in enumerate((saved, grads)):
        for i in range(cuts):
            at = pl.ds(tall * i, tall)
            copies.append(pltpu.make_async_copy(ref.at[0, at], held.at[k, at], sems.at[k, i]))
    for copy in copies:
        copy.start()
    starts, lives, slots = recall(info, 1)
    total = jnp.sum(parts[...].astype(F32), axis=0)
    back_rank = total[:rank].astype(BF16)
    back_grad = (ADAPTER_SCALE * total[rank:]).astype(BF16)
    count, _, width = out.shape
    row = lax.broadcasted_iota(jnp.int32, (rank, width), 0)
    notes = ahead[wide:, :width].astype(F32)
    for i in range(SEGS):
        notes = jnp.where(row == i, slots[i].astype(F32), notes)
    lefts = (
        spread(back_grad, alive_rows(starts, lives, 0, length)),
        spread(back_rank, note_masks(ahead, wide, length)),
    )
    for d in range(count):
        out[d, 2 * wide :, :] = notes.astype(BF16)
    for k, left in enumerate(lefts):
        for copy in copies[cuts * k : cuts * (k + 1)]:
            copy.wait()
        full = jnp.dot(left, held[k], preferred_element_type=F32).astype(BF16)
        for d in range(count):
            out[d, wide * k : wide * (k + 1), :] = full[:, width * d : width * (d + 1)]


def collect(pieces, half, scale, rows):
    count, _, width = pieces.shape
    rank = pieces.shape[1] // (2 * SEGS + 1)
    wide = SEGS * rank
    slot_at = lax.broadcasted_iota(jnp.int32, (rows // rank, 1, width), 0).astype(F32)
    total = jnp.zeros((rows // rank, rank, width), F32)
    for d in range(count):
        notes = pieces[d, 2 * wide :, :].astype(F32)
        for i in range(SEGS):
            slot = notes[half * SEGS + i : half * SEGS + i + 1]
            first = half * wide + rank * i
            piece = pieces[d, first : first + rank, :].astype(F32)
            total = total + jnp.where(slot_at == slot[None], piece[None], 0.0)
    return (scale * total).reshape(rows, width).astype(BF16)


def collect_up_kernel(pieces, out):
    out[...] = collect(pieces, 1, ADAPTER_SCALE, out.shape[0])


def copy_to_all(block, out, first, sems):
    rows = block.shape[0]
    copies = [
        pltpu.make_async_copy(block, out.at[d, pl.ds(first, rows)], sems.at[d]) for d in range(out.shape[0])
    ]
    for copy in copies:
        copy.start()
    for copy in copies:
        copy.wait()


def collect_down_kernel(pieces, out, block, sems):
    block[...] = collect(pieces, 0, 1.0, block.shape[0])
    copy_to_all(block, out, 0, sems)


def add_up_kernel(block, half, out, sems):
    del half
    copy_to_all(block, out, block.shape[0], sems)


def unpack_kernel(sums, down_out, up_out):
    count, rows, width = sums.shape
    for half, ref in enumerate((down_out, up_out)):
        _, slots, rank, _ = ref.shape
        for d in range(count):
            block = sums[d, half * (rows // 2) : (half + 1) * (rows // 2)]
            ref[0, :, :, width * d : width * (d + 1)] = block.reshape(slots, rank, width)


def hand_on_kernel(info, arrived, fwd, up, out):
    rows = out.shape[1]
    first = pl.multiple_of(pl.program_id(0) * rows, rows)
    starts, lives, slots = recall(info, 0)
    wide = spread(fwd[:, pl.ds(first, rows)], alive_rows(starts, lives, first, rows))
    update = lax.dot_general(
        wide, pick_rows(up, slots), (((0,), (0,)), ((), ())), preferred_element_type=F32
    )
    out[0] = (arrived[0].astype(F32) + ADAPTER_SCALE * update).astype(BF16)


def in_hbm(value):
    return pltpu.with_memory_space_constraint(value, pltpu.HBM)


def shift(value, steps):
    count = lax.axis_size("section")
    return lax.ppermute(value, "section", [(i, (i + steps) % count) for i in range(count)])


def exchange_add(value, distance):
    count = lax.axis_size(TENSOR)
    return value + lax.ppermute(value, TENSOR, [(i, i ^ distance) for i in range(count)])


def per_device(
    act_inbox,
    grad_inbox,
    queries,
    keys_values,
    saved_attn,
    down_adapt,
    up_adapt,
    seg_blocks,
    seg_pads,
    seg_tenant,
    adapter_table,
):
    _, length, width = act_inbox.shape
    _, slot_count, rank, _ = up_adapt.shape
    wide = SEGS * rank
    scalars = (seg_blocks, seg_pads, seg_tenant, adapter_table)
    dp_count = lax.axis_size("dp")
    part = width // dp_count
    piece = length * width * 2

    vmem = lambda shape: pltpu.VMEM(shape, BF16)
    ahead, info = pl.pallas_call(
        prepare_kernel,
        out_shape=(vmem((wide + rank, width)), jax.ShapeDtypeStruct((1, 2 * SEGS * SEGS), jnp.int32)),
        in_specs=[HBM] * 7,
        out_specs=(VMEM, SMEM),
        scratch_shapes=[
            pltpu.SMEM((3, *seg_blocks.shape), jnp.int32),
            pltpu.SMEM(adapter_table.shape, jnp.int32),
            pltpu.VMEM((length, width), BF16),
            pltpu.VMEM(down_adapt.shape, BF16),
            pltpu.VMEM(up_adapt.shape, BF16),
            pltpu.SemaphoreType.DMA((7,)),
        ],
        compiler_params=PARAMS,
        cost_estimate=cost(2 * wide * length * width, 5 * piece),
        name="prepare",
    )(*[in_hbm(x) for x in (*scalars, saved_attn, down_adapt, up_adapt)])
    theirs = shift(ahead, 1)

    attention_cost = cost(
        2 * length * MOST_BLOCKS * BLOCK * width + wide * length * width,
        piece * 3 // 4,
        length * MOST_BLOCKS * BLOCK * width // HD // 2,
    )
    half = length // 2
    early = pl.pallas_call(
        early_attention_kernel,
        out_shape=pltpu.VMEM((rank, half), F32),
        in_specs=[SMEM] + [VMEM] * 3,
        out_specs=VMEM,
        scratch_shapes=[pltpu.VMEM((half, width), BF16)],
        compiler_params=PARAMS,
        cost_estimate=attention_cost,
        name="early_attention",
    )(info, queries, keys_values, down_adapt)
    theirs, early, act_inbox = lax.optimization_barrier((theirs, early, act_inbox))
    arrived = shift(act_inbox, 1)

    grad_part = pl.pallas_call(
        back_gradient_kernel,
        out_shape=pltpu.VMEM((rank, length), F32),
        in_specs=[VMEM] * 2,
        out_specs=VMEM,
        compiler_params=PARAMS,
        cost_estimate=cost(2 * wide * length * width, piece),
        name="back_gradient",
    )(theirs, grad_inbox)
    grad_part = shift(grad_part, -1)

    def copies(value, count):
        return jnp.broadcast_to(value[None], (count, *value.shape))

    back = theirs[wide:, length : 2 * length].astype(F32) + theirs[wide:, 2 * length : 3 * length].astype(F32)
    parts = jnp.concatenate([back, grad_part], axis=0)
    queries, parts = lax.optimization_barrier((queries, parts))
    parts = exchange_add(parts, 4).astype(BF16)
    late = pl.pallas_call(
        late_attention_kernel,
        out_shape=pltpu.VMEM((rank, half), F32),
        in_specs=[SMEM] + [VMEM] * 3,
        out_specs=VMEM,
        scratch_shapes=[pltpu.VMEM((half, width), BF16)],
        compiler_params=PARAMS,
        cost_estimate=attention_cost,
        name="late_attention",
    )(info, queries, keys_values, down_adapt)
    parts, late = lax.optimization_barrier((parts, late))
    parts = lax.all_to_all(copies(parts, lax.axis_size("zi")), "zi", 0, 0)

    fwd_sum = exchange_add(jnp.concatenate([early, late], axis=1), 1)

    pieces = pl.pallas_call(
        contract_kernel,
        out_shape=jax.ShapeDtypeStruct((dp_count, 2 * wide + rank, part), BF16),
        in_specs=[SMEM, VMEM, VMEM, HBM, HBM],
        out_specs=VMEM,
        scratch_shapes=[
            pltpu.VMEM((2, length, width), BF16),
            pltpu.SemaphoreType.DMA((2, 4)),
        ],
        compiler_params=PARAMS,
        cost_estimate=cost(4 * wide * length * width, 2 * piece),
        name="contract",
    )(info, parts, theirs, in_hbm(saved_attn), in_hbm(grad_inbox))
    pieces, fwd_sum = lax.optimization_barrier((pieces, fwd_sum))
    fwd_sum = exchange_add(fwd_sum, 2)
    pieces = lax.all_to_all(pieces, "dp", 0, 0)
    pieces, fwd_sum = lax.optimization_barrier((pieces, fwd_sum))

    rows = slot_count * rank
    up_sum = pl.pallas_call(
        collect_up_kernel,
        out_shape=vmem((rows, part)),
        in_specs=[VMEM],
        out_specs=VMEM,
        compiler_params=PARAMS,
        cost_estimate=cost(2 * dp_count * SEGS * rows * part, piece // 4),
        name="collect_up",
    )(pieces)
    pieces, up_sum = lax.optimization_barrier((pieces, up_sum))
    sums_shape = jax.ShapeDtypeStruct((dp_count, 2 * rows, part), BF16)
    sums = pl.pallas_call(
        collect_down_kernel,
        out_shape=sums_shape,
        in_specs=[VMEM],
        out_specs=HBM,
        scratch_shapes=[pltpu.VMEM((rows, part), BF16), pltpu.SemaphoreType.DMA((dp_count,))],
        compiler_params=PARAMS,
        cost_estimate=cost(2 * dp_count * SEGS * rows * part, piece // 2),
        name="collect_down",
    )(pieces)
    sums = pl.pallas_call(
        add_up_kernel,
        out_shape=sums_shape,
        in_specs=[VMEM, HBM],
        out_specs=HBM,
        scratch_shapes=[pltpu.SemaphoreType.DMA((dp_count,))],
        input_output_aliases={1: 0},
        compiler_params=PARAMS,
        cost_estimate=cost(0, piece // 4),
        name="add_up",
    )(shift(up_sum, -1), sums)
    sums, arrived, fwd_sum = lax.optimization_barrier((sums, arrived, fwd_sum))
    fwd_sum = exchange_add(fwd_sum, 4)
    sums = lax.all_to_all(sums, "dp", 0, 0)

    rows = 128
    new_acts = pl.pallas_call(
        hand_on_kernel,
        grid=(length // rows,),
        out_shape=jax.ShapeDtypeStruct(act_inbox.shape, BF16),
        in_specs=[SMEM, pl.BlockSpec((1, rows, width), lambda i: (0, i, 0)), VMEM, VMEM],
        out_specs=pl.BlockSpec((1, rows, width), lambda i: (0, i, 0)),
        compiler_params=PARAMS,
        cost_estimate=cost(2 * wide * length * width, 2 * piece),
        name="hand_on",
    )(info, arrived, fwd_sum, up_adapt)

    sums, new_acts = lax.optimization_barrier((sums, new_acts))
    grad_down, grad_up = pl.pallas_call(
        unpack_kernel,
        out_shape=(jax.ShapeDtypeStruct(up_adapt.shape, BF16),) * 2,
        in_specs=[VMEM],
        out_specs=(VMEM, VMEM),
        compiler_params=PARAMS,
        cost_estimate=cost(0, piece),
        name="unpack",
    )(sums)
    return new_acts, grad_down, grad_up


def solution(mesh):
    section, tensor, dp = (mesh.shape[name] for name in ("section", "tensor", "dp"))
    fine = jax.sharding.Mesh(mesh.devices.reshape(section, 2, tensor // 2, dp), ("section", *TENSOR, "dp"))
    rows = P("section", "dp", TENSOR)
    adapters = P("section", None, None, TENSOR)
    scalars = P("section", None, "dp", None)
    return jax.shard_map(
        per_device,
        mesh=fine,
        in_specs=(
            rows,
            rows,
            rows,
            P("section", None, "dp", TENSOR),
            rows,
            adapters,
            adapters,
            scalars,
            scalars,
            scalars,
            P(),
        ),
        out_specs=(rows, adapters, adapters),
        check_vma=False,
    )
```
